128 devices in a mesh: attn: 16 (over z, x), expert: 8 (over y, core).
Axes of the slice: x: 4, y: 4, z: 4, core: 2. Of those that a mesh axis runs over, the one named last changes fastest.
Arguments:
- resid: bfloat16 [1024, 6144], P('attn', 'expert')
- query: bfloat16 [1024, 6144], P('attn', 'expert'), may hold values from -1 to 1
- key_cache: bfloat16 [1024, 8, 128, 128], P('attn', 'expert'), may hold values from -4 to 4
- value_cache: bfloat16 [1024, 8, 128, 128], P('attn', 'expert'), may hold values from -6 to 6
- new_key: bfloat16 [1024, 1024], P('attn', 'expert'), may hold values from -4 to 4
- new_value: bfloat16 [1024, 1024], P('attn', 'expert'), may hold values from -6 to 6
- lengths: int32 [1024], P('attn'), may hold values from 1 to 128, as said below
- norm_gain: float32 [6144], P('expert'), may hold values from 0.1 to 1.9
- router_weight: float32 [6144, 8], P('expert'), may hold values from -0.078125 to 0.078125
- expert_ids: int32 [1024, 2], P('attn'), may hold values from 0 to 7, as said below
- w_gate: bfloat16 [8, 6144, 8192], P('expert', None, 'attn'), may hold values from -0.078125 to 0.078125
- w_up: bfloat16 [8, 6144, 8192], P('expert', None, 'attn'), may hold values from -0.078125 to 0.078125
- w_down: bfloat16 [8, 8192, 6144], P('expert', 'attn'), may hold values from -0.0625 to 0.0625
Outputs:
- layer_out: bfloat16 [1024, 6144], P('attn', 'expert')
The draws below stay inside these ranges and needn't reach their ends.
Inputs may be any that keep to these rules, and one draw needn't show every extreme that they name: `expert_ids`: each row names two different experts. Within each aligned block of 64 rows (the rows of one index of attn) no expert is named by more than 32 rows, and one expert, the same in every block, is named by exactly 32 rows in each block. `lengths`: some row has all 128 positions filled and some row has one.
All inputs are finite; a program needn't handle non-finite values.
Results may differ from the reference program's by a relative error of at most 0.0095.
Values may be sent and summed in bfloat16 or wider, within the bound.
No kernel may reach another device: no remote copies, remote signals or barrier semaphores. Data moves between devices by JAX's collectives and lax.ppermute only.
A program may use at most 128 MiB of HBM per device.

```python
import math
import jax
import jax.numpy as jnp
from jax import lax

D = 6144
HQ = 48
KVH = 8
HD = 128
E = 8
FF = 8192
R_DEV = 64
CACHE = 128
CAP = 32
ROWS = 1024
N_ATTN = 16


def draw_resid(key, part):
    key_base, key_rows, key_cols = jax.random.split(key, 3)
    position = jnp.arange(D, dtype=jnp.float32)[None, :] / (D - 1)
    base = jnp.clip(jax.random.normal(key_base, (ROWS, D), jnp.float32), -6.0, 6.0)
    rising = jnp.exp(position * math.log(3.0))
    row_scale = jnp.exp(jax.random.uniform(key_rows, (ROWS, 1), jnp.float32, math.log(0.5), math.log(2.0)))
    factor = 0.15
    spread = jnp.exp(jax.random.uniform(key_cols, (1, D), jnp.float32, 0.0, math.log(3.4)))
    return (factor * base * rising * spread * row_scale).astype(jnp.bfloat16)


def draw_lengths(key, part):
    key_all, key_full, key_short = jax.random.split(key, 3)
    filled = jax.random.randint(key_all, (ROWS,), 1, CACHE + 1)
    full_row = jax.random.randint(key_full, (), 0, ROWS)
    short_row = (full_row + 1 + jax.random.randint(key_short, (), 0, ROWS - 1)) % ROWS
    filled = filled.at[full_row].set(CACHE)
    filled = filled.at[short_row].set(1)
    return filled.astype(jnp.int32)


def draw_expert_ids(key, part):
    key_hot, key_rows, key_order, key_flip = jax.random.split(key, 4)
    block_count = ROWS // R_DEV
    hot_expert = jax.random.randint(key_hot, (), 0, E)
    position = jax.vmap(lambda sub_key: jax.random.permutation(sub_key, R_DEV))(jax.random.split(key_rows, block_count))
    ordering = jax.vmap(lambda sub_key: jax.random.permutation(sub_key, E - 1))(jax.random.split(key_order, block_count))
    others = ordering + (ordering >= hot_expert).astype(jnp.int32)
    first_other = jnp.take_along_axis(others, position % (E - 1), axis=1)
    next_other = jnp.take_along_axis(others, (position + 1) % (E - 1), axis=1)
    leading = position < CAP
    choice_one = jnp.where(leading, hot_expert, first_other)
    choice_two = jnp.where(leading, first_other, next_other)
    flipped = jax.random.randint(key_flip, (block_count, R_DEV), 0, 2) == 1
    column_a = jnp.where(flipped, choice_two, choice_one)
    column_b = jnp.where(flipped, choice_one, choice_two)
    return jnp.stack([column_a, column_b], axis=-1).reshape(ROWS, 2).astype(jnp.int32)


def steps_of(own_key, shape, shards, low, high):
    factor_of = 1.0
    for dim, parts in shards:
        steps = jax.random.uniform(jax.random.fold_in(jax.random.fold_in(own_key, 6), dim), (parts,), jnp.float32, low / len(shards), high / len(shards))
        factor_of = factor_of * jnp.repeat(jnp.exp(steps), shape[dim] // parts).reshape((-1,) + (1,) * (len(shape) - 1 - dim))
    return factor_of


def centred(stream_key, shape, scale, bound, pieces=(), held_as=jnp.bfloat16):
    values = scale * jax.random.normal(stream_key, shape, jnp.float32)
    if pieces:
        values = values * steps_of(stream_key, shape, pieces, -0.22, 0.18)
    return jnp.clip(values, -bound, bound).astype(held_as)


def setup_inputs(seed: int = 0) -> dict:
    splits = jax.random.split(jax.random.key(seed), 14)
    return {
        "resid": draw_resid(jax.random.fold_in(splits[13], 71), 0),
        "query": jnp.clip(jax.random.uniform(splits[1], (ROWS, D), jnp.float32, -1.0, 1.0) * steps_of(splits[1], (ROWS, D), ((0, 16), (1, 8)), -0.4, 0.0), -1.0, 1.0).astype(jnp.bfloat16),
        "key_cache": centred(splits[2], (ROWS, KVH, CACHE, HD), 1.0, 4.0, ((0, 16), (1, 8))),
        "value_cache": centred(splits[3], (ROWS, KVH, CACHE, HD), 1.0, 6.0, ((0, 16), (1, 8))),
        "new_key": centred(splits[4], (ROWS, KVH * HD), 1.0, 4.0, ((0, 16), (1, 8))),
        "new_value": centred(splits[5], (ROWS, KVH * HD), 1.0, 6.0, ((0, 16), (1, 8))),
        "lengths": draw_lengths(jax.random.fold_in(splits[13], 71), 0),
        "norm_gain": jnp.clip(1.0 + 0.18 * jax.random.normal(splits[7], (D,), jnp.float32), 0.1, 1.9),
        "router_weight": centred(splits[8], (D, E), D ** -0.5, 0.078125, ((0, 8),), jnp.float32),
        "expert_ids": draw_expert_ids(jax.random.fold_in(splits[13], 71), 0),
        "w_gate": centred(splits[10], (E, D, FF), D ** -0.5, 0.078125, ((0, 8), (2, 16))),
        "w_up": centred(splits[11], (E, D, FF), D ** -0.5, 0.078125, ((0, 8), (2, 16))),
        "w_down": centred(splits[12], (E, FF, D), FF ** -0.5, 0.0625, ((0, 8), (1, 16))),
    }


EPSILON = 1e-05

def reference(resid, query, key_cache, value_cache, new_key, new_value, lengths, norm_gain, router_weight, expert_ids, w_gate, w_up, w_down):
    row_count = resid.shape[0]
    group_size = HQ // KVH
    score_scale = 1.0 / math.sqrt(HD)
    queries = query.astype(jnp.float32).reshape(row_count, KVH, group_size, HD)
    scores = jnp.einsum('rkgd,rkld->rkgl', queries, key_cache.astype(jnp.float32)) * score_scale
    fresh_score = jnp.einsum('rkgd,rkd->rkg', queries, new_key.astype(jnp.float32).reshape(row_count, KVH, HD)) * score_scale
    usable = jnp.arange(CACHE, dtype=jnp.int32)[None, :] < lengths[:, None]
    powers = jnp.where(usable[:, None, None, :], jnp.exp(scores), jnp.float32(0.0))
    fresh_power = jnp.exp(fresh_score)
    denominator = lax.optimization_barrier(jnp.sum(powers, axis=-1)) + fresh_power
    weights_cache = (powers / denominator[..., None]).astype(jnp.bfloat16)
    weight_fresh = (fresh_power / denominator).astype(jnp.bfloat16)
    attended = jnp.einsum('rkgl,rkld->rkgd', weights_cache.astype(jnp.float32), value_cache.astype(jnp.float32))
    attended = attended + weight_fresh.astype(jnp.float32)[..., None] * new_value.astype(jnp.float32).reshape(row_count, KVH, 1, HD)
    hidden_state = resid.astype(jnp.float32) + attended.reshape(row_count, D)
    mean_square = lax.optimization_barrier(jnp.mean(hidden_state * hidden_state, axis=1, keepdims=True))
    normed = hidden_state * lax.rsqrt(mean_square + EPSILON) * norm_gain
    narrow = normed.astype(jnp.bfloat16)
    logits = jnp.dot(normed, router_weight, precision=lax.Precision.HIGHEST)
    choose = expert_ids[:, :, None] == jnp.arange(E, dtype=jnp.int32)[None, None, :]
    picked = lax.optimization_barrier(jnp.sum(jnp.where(choose, logits[:, None, :], jnp.float32(0.0)), axis=2))
    first_weight = 1.0 / (1.0 + jnp.exp(picked[:, 1] - picked[:, 0]))
    second_weight = 1.0 / (1.0 + jnp.exp(picked[:, 0] - picked[:, 1]))
    hits = lax.optimization_barrier(jnp.sum(choose.astype(jnp.int32), axis=1)).reshape(row_count // R_DEV, R_DEV, E)
    before = (jnp.cumsum(hits, axis=1) - hits).reshape(row_count, E)
    slot_index = lax.optimization_barrier(jnp.sum(jnp.where(choose, before[:, None, :], 0), axis=2)).astype(jnp.int32)
    block_index = (jnp.arange(row_count, dtype=jnp.int32) // R_DEV)[:, None]
    destination = (block_index * CAP + slot_index).astype(jnp.int32)
    owner = jnp.broadcast_to(jnp.arange(row_count, dtype=jnp.int32)[:, None], (row_count, 2))
    table = jnp.zeros((E, N_ATTN * CAP), jnp.int32).at[expert_ids, destination].set(owner)
    group_width = FF // N_ATTN

    def run_expert(packed):
        gate_matrix, up_matrix, down_matrix, row_index = packed
        taken = narrow[row_index]
        gate_part = jnp.dot(taken, gate_matrix, preferred_element_type=jnp.float32)
        up_part = jnp.dot(taken, up_matrix, preferred_element_type=jnp.float32)
        activation = (jax.nn.silu(gate_part) * up_part).astype(jnp.bfloat16)
        total = jnp.zeros((taken.shape[0], D), jnp.float32)
        for group in range(N_ATTN):
            partial_value = jnp.dot(activation[:, group * group_width:(group + 1) * group_width], down_matrix[group * group_width:(group + 1) * group_width], preferred_element_type=jnp.float32)
            total = total + partial_value.astype(jnp.bfloat16).astype(jnp.float32)
        return total.astype(jnp.bfloat16)
    outputs = lax.map(run_expert, (w_gate, w_up, w_down, table))
    first_out = outputs[expert_ids[:, 0], destination[:, 0]].astype(jnp.float32)
    second_out = outputs[expert_ids[:, 1], destination[:, 1]].astype(jnp.float32)
    total = hidden_state + first_weight[:, None] * first_out + second_weight[:, None] * second_out
    return total.astype(jnp.bfloat16)
```

```python
import math

import jax
import jax.numpy as jnp
from jax import lax
from jax.sharding import PartitionSpec as P

D = 6144
E = 8
CAP = 32
SIDE = 4
HALF = CAP // 2


EPSILON = 1e-05


def shift_z(value, step):
    pairs = [
        (z * SIDE + x, ((z + step) % SIDE) * SIDE + x) for z in range(SIDE) for x in range(SIDE)
    ]
    return lax.ppermute(value, "attn", pairs)


def shift_x(value, step):
    pairs = [
        (z * SIDE + x, z * SIDE + (x + step) % SIDE) for z in range(SIDE) for x in range(SIDE)
    ]
    return lax.ppermute(value, "attn", pairs)


def spread_near(block, shift):
    return shift(block, 1), shift(block, -1)


def spread_far(behind, ahead, shift):
    half = behind.shape[0] // 2
    return jnp.concatenate([shift(behind[:half], 1), shift(ahead[half:], -1)], axis=0)


def split_three(value):
    high = value.astype(jnp.bfloat16)
    rest = value - high.astype(jnp.float32)
    middle = rest.astype(jnp.bfloat16)
    low = (rest - middle.astype(jnp.float32)).astype(jnp.bfloat16)
    return [high, middle, low]


def ring_sum(behind, own, ahead, far, shift):
    half = far.shape[0] // 2
    sent = far.astype(jnp.bfloat16)
    far_up = shift(sent[:half], 1).astype(jnp.float32)
    far_down = shift(sent[half:], -1).astype(jnp.float32)
    up = jnp.concatenate([ahead[:half] + far_up, ahead[half:]], axis=0)
    down = jnp.concatenate([behind[:half], behind[half:] + far_down], axis=0)
    got_up = shift(up.astype(jnp.bfloat16), 1).astype(jnp.float32)
    got_down = shift(down.astype(jnp.bfloat16), -1).astype(jnp.float32)
    return own + got_up + got_down


def on_device(
    resid,
    query,
    key_cache,
    value_cache,
    new_key,
    new_value,
    lengths,
    norm_gain,
    router_weight,
    expert_ids,
    w_gate,
    w_up,
    w_down,
):
    row_count = resid.shape[0]
    width_local = resid.shape[1]
    kv_local = key_cache.shape[1]
    cache_slots = key_cache.shape[2]
    head_size = key_cache.shape[3]
    group_size = query.shape[1] // (kv_local * head_size)
    expert_devices = lax.axis_size("expert")
    score_scale = 1.0 / math.sqrt(head_size)
    queries = query.reshape(row_count, kv_local, group_size, head_size)
    scores = (
        jnp.einsum("rkgd,rkld->rkgl", queries, key_cache, preferred_element_type=jnp.float32)
        * score_scale
    )
    fresh_score = (
        jnp.einsum(
            "rkgd,rkd->rkg",
            queries,
            new_key.reshape(row_count, kv_local, head_size),
            preferred_element_type=jnp.float32,
        )
        * score_scale
    )
    usable = lax.broadcasted_iota(jnp.int32, (row_count, cache_slots), 1) < lengths[:, None]
    powers = jnp.where(usable[:, None, None, :], jnp.exp(scores), jnp.float32(0.0))
    fresh_power = jnp.exp(fresh_score)
    denominator = jnp.sum(powers, axis=-1) + fresh_power
    weights_cache = (powers / denominator[..., None]).astype(jnp.bfloat16)
    weight_fresh = (fresh_power / denominator).astype(jnp.bfloat16)
    attended = jnp.einsum(
        "rkgl,rkld->rkgd", weights_cache, value_cache, preferred_element_type=jnp.float32
    )
    attended = attended + weight_fresh.astype(jnp.float32)[..., None] * new_value.astype(
        jnp.float32
    ).reshape(row_count, kv_local, 1, head_size)
    hidden_state = resid.astype(jnp.float32) + attended.reshape(row_count, width_local)

    gained = hidden_state * norm_gain
    sums = jnp.concatenate(
        [
            jnp.sum(hidden_state * hidden_state, axis=1, keepdims=True),
            jnp.dot(gained, router_weight, precision=lax.Precision.HIGHEST),
        ],
        axis=1,
    )
    pieces = split_three(sums)
    columns = sums.shape[1]
    payload = jnp.concatenate(
        [gained.astype(jnp.bfloat16)]
        + pieces
        + [jnp.zeros((row_count, 128 - 3 * columns), jnp.bfloat16)],
        axis=1,
    )
    gathered = lax.all_gather(payload, "expert", axis=0)
    whole_rows = gathered[:, :, :width_local]
    side = gathered[:, :, width_local:].astype(jnp.float32)
    sums = jnp.sum(
        side[:, :, :columns] + side[:, :, columns : 2 * columns] + side[:, :, 2 * columns : 3 * columns],
        axis=0,
    )
    scale = lax.rsqrt(sums[:, :1] / D + EPSILON)
    logits = sums[:, 1:] * scale

    choose = expert_ids[:, :, None] == lax.broadcasted_iota(jnp.int32, (1, 1, E), 2)
    picked = jnp.sum(jnp.where(choose, logits[:, None, :], jnp.float32(0.0)), axis=2)
    first_weight = 1.0 / (1.0 + jnp.exp(picked[:, 1] - picked[:, 0]))
    second_weight = 1.0 / (1.0 + jnp.exp(picked[:, 0] - picked[:, 1]))
    hits = jnp.sum(choose.astype(jnp.int32), axis=1)
    before = jnp.cumsum(hits, axis=0) - hits
    slot_index = jnp.sum(jnp.where(choose, before[:, None, :], 0), axis=2)
    own_expert = lax.axis_index("expert")
    own_slot = jnp.sum(jnp.where(expert_ids == own_expert, slot_index + 1, 0), axis=1) - 1
    own_selector = (
        lax.broadcasted_iota(jnp.int32, (CAP, row_count), 0) == own_slot[None, :]
    )
    outgoing = jnp.einsum(
        "cr,erd->ced",
        own_selector.astype(jnp.bfloat16),
        whole_rows,
        preferred_element_type=jnp.float32,
    ).reshape(CAP, D)
    own_scale = jnp.sum(
        jnp.where(own_selector, scale[:, 0][None, :], jnp.float32(0.0)), axis=1, keepdims=True
    )
    outgoing = (outgoing * own_scale).astype(jnp.bfloat16)

    gate_weight = w_gate[0]
    up_weight = w_up[0]
    down_weight = w_down[0]

    def feed(rows):
        gate_part = jnp.dot(rows, gate_weight, preferred_element_type=jnp.float32)
        up_part = jnp.dot(rows, up_weight, preferred_element_type=jnp.float32)
        activation = (jax.nn.silu(gate_part) * up_part).astype(jnp.bfloat16)
        return jnp.dot(activation, down_weight, preferred_element_type=jnp.float32)

    a_own, b_own = outgoing[:HALF], outgoing[HALF:]
    a_behind, a_ahead = spread_near(a_own, shift_z)
    b_behind, b_ahead = spread_near(b_own, shift_x)
    a_far = spread_far(a_behind, a_ahead, shift_z)
    b_far = spread_far(b_behind, b_ahead, shift_x)
    a_line = jnp.concatenate([a_own, a_behind, a_ahead, a_far], axis=0)
    b_line = jnp.concatenate([b_own, b_behind, b_ahead, b_far], axis=0)
    line = a_line.shape[0]
    aa_behind, aa_ahead = spread_near(a_line, shift_x)
    bb_behind, bb_ahead = spread_near(b_line, shift_z)
    aa_far = spread_far(aa_behind, aa_ahead, shift_x)
    bb_far = spread_far(bb_behind, bb_ahead, shift_z)

    part_own = feed(jnp.concatenate([a_line, b_line], axis=0))
    part_near = feed(jnp.concatenate([aa_behind, bb_behind, aa_ahead, bb_ahead], axis=0))
    part_far = feed(jnp.concatenate([aa_far, bb_far], axis=0))

    a_sum = ring_sum(
        part_near[:line], part_own[:line], part_near[2 * line : 3 * line], part_far[:line], shift_x
    )
    b_sum = ring_sum(
        part_near[line : 2 * line], part_own[line:], part_near[3 * line :], part_far[line:], shift_z
    )
    a_result = ring_sum(
        a_sum[HALF : 2 * HALF], a_sum[:HALF], a_sum[2 * HALF : 3 * HALF], a_sum[3 * HALF :], shift_z
    )
    b_result = ring_sum(
        b_sum[HALF : 2 * HALF], b_sum[:HALF], b_sum[2 * HALF : 3 * HALF], b_sum[3 * HALF :], shift_x
    )
    expert_result = jnp.concatenate([a_result, b_result], axis=0).astype(jnp.bfloat16)

    expert_result = expert_result.reshape(CAP, 1, expert_devices, width_local)
    returned = lax.all_to_all(expert_result, "expert", split_axis=2, concat_axis=1, tiled=True)
    flat_result = returned.reshape(CAP * E, width_local)
    target_index = slot_index * E + expert_ids
    picker = (
        target_index[:, :, None] == lax.broadcasted_iota(jnp.int32, (1, 1, CAP * E), 2)
    ).astype(jnp.bfloat16)
    taken = jnp.einsum("rkm,md->krd", picker, flat_result, preferred_element_type=jnp.float32)
    total = hidden_state + first_weight[:, None] * taken[0] + second_weight[:, None] * taken[1]
    return total.astype(jnp.bfloat16)


def solution(mesh):
    return jax.shard_map(
        on_device,
        mesh=mesh,
        in_specs=(
            P("attn", "expert"),
            P("attn", "expert"),
            P("attn", "expert", None, None),
            P("attn", "expert", None, None),
            P("attn", "expert"),
            P("attn", "expert"),
            P("attn"),
            P("expert"),
            P("expert", None),
            P("attn", None),
            P("expert", None, "attn"),
            P("expert", None, "attn"),
            P("expert", "attn", None),
        ),
        out_specs=P("attn", "expert"),
        check_vma=False,
    )
```

```python
import functools
import math

import jax
import jax.numpy as jnp
from jax import lax
from jax.experimental import pallas as pl
from jax.experimental.pallas import tpu as pltpu
from jax.sharding import PartitionSpec as P

D = 6144
E = 8
CAP = 32
SIDE = 4
HALF = CAP // 2


EPSILON = 1e-05


def ring_pairs(step, second):
    pairs = []
    for z in range(SIDE):
        for x in range(SIDE):
            for y in range(SIDE):
                for core in range(2):
                    along_z = (core == 0) != second
                    to_z = (z + step) % SIDE if along_z else z
                    to_x = x if along_z else (x + step) % SIDE
                    source = (z * SIDE + x) * E + y * 2 + core
                    target = (to_z * SIDE + to_x) * E + y * 2 + core
                    pairs.append((source, target))
    return pairs


def shift_first(value, step):
    return lax.ppermute(value, ("attn", "expert"), ring_pairs(step, False))


def shift_second(value, step):
    return lax.ppermute(value, ("attn", "expert"), ring_pairs(step, True))


def split_three(value):
    high = value.astype(jnp.bfloat16)
    rest = value - high.astype(jnp.float32)
    middle = rest.astype(jnp.bfloat16)
    low = (rest - middle.astype(jnp.float32)).astype(jnp.bfloat16)
    return [high, middle, low]


def add_rounded(one, other):
    return (one.astype(jnp.float32) + other.astype(jnp.float32)).astype(jnp.bfloat16)


def ring_sum(behind, own, ahead, far_low, far_high, shift):
    half = far_low.shape[0]
    got_low = shift(far_low, 1)
    got_high = shift(far_high, -1)
    up = jnp.concatenate([add_rounded(ahead[:half], got_low), ahead[half:]], axis=0)
    down = jnp.concatenate([behind[:half], add_rounded(behind[half:], got_high)], axis=0)
    from_behind = shift(up, 1)
    from_ahead = shift(down, -1)
    return (
        own.astype(jnp.float32) + from_behind.astype(jnp.float32) + from_ahead.astype(jnp.float32)
    )


K_BLOCK = 1536
N_BLOCK = 1536


def feed_kernel(count, steps_in, *refs):
    row_refs = refs[:count]
    gate_ref, up_ref, down_ref, out_ref, rows, gate_sum, up_sum, active = refs[count:]
    step = pl.program_id(0)

    @pl.when(step == 0)
    def _():
        at = 0
        for ref in row_refs:
            rows[at : at + ref.shape[0], :] = ref[...]
            at += ref.shape[0]

    @pl.when(step < steps_in)
    def _():
        part = rows[:, pl.ds(pl.multiple_of(step * K_BLOCK, 128), K_BLOCK)]
        gate_part = jnp.dot(part, gate_ref[0], preferred_element_type=jnp.float32)
        up_part = jnp.dot(part, up_ref[0], preferred_element_type=jnp.float32)

        @pl.when(step == 0)
        def _():
            gate_sum[...] = gate_part
            up_sum[...] = up_part

        @pl.when(step > 0)
        def _():
            gate_sum[...] += gate_part
            up_sum[...] += up_part

    @pl.when(step == steps_in - 1)
    def _():
        active[...] = (jax.nn.silu(gate_sum[...]) * up_sum[...]).astype(jnp.bfloat16)

    @pl.when(step >= steps_in)
    def _():
        out_ref[...] = jnp.dot(
            active[...], down_ref[0], preferred_element_type=jnp.float32
        ).astype(jnp.bfloat16)


def feed(row_arrays, w_gate, w_up, w_down):
    count = sum(array.shape[0] for array in row_arrays)
    width, hidden = w_gate.shape[1:]
    steps_in = width // K_BLOCK
    steps_out = width // N_BLOCK
    return pl.pallas_call(
        functools.partial(feed_kernel, len(row_arrays), steps_in),
        grid=(steps_in + steps_out,),
        in_specs=[
            pl.BlockSpec(array.shape, lambda i: (0, 0), pipeline_mode=pl.Buffered(1))
            for array in row_arrays
        ]
        + [
            pl.BlockSpec((1, K_BLOCK, hidden), lambda i: (0, jnp.minimum(i, steps_in - 1), 0)),
            pl.BlockSpec((1, K_BLOCK, hidden), lambda i: (0, jnp.minimum(i, steps_in - 1), 0)),
            pl.BlockSpec((1, hidden, N_BLOCK), lambda i: (0, 0, jnp.maximum(i - steps_in, 0))),
        ],
        out_specs=pl.BlockSpec((count, N_BLOCK), lambda i: (0, jnp.maximum(i - steps_in, 0))),
        out_shape=jax.ShapeDtypeStruct((count, width), jnp.bfloat16),
        scratch_shapes=[
            pltpu.VMEM((count, width), jnp.bfloat16),
            pltpu.VMEM((count, hidden), jnp.float32),
            pltpu.VMEM((count, hidden), jnp.float32),
            pltpu.VMEM((count, hidden), jnp.bfloat16),
        ],
        compiler_params=pltpu.CompilerParams(vmem_limit_bytes=30 * 1024 * 1024),
        cost_estimate=pl.CostEstimate(
            flops=6 * count * width * hidden,
            bytes_accessed=6 * width * hidden + 4 * count * width,
            transcendentals=count * hidden,
        ),
    )(*row_arrays, w_gate, w_up, w_down)


def on_device(
    resid,
    query,
    key_cache,
    value_cache,
    new_key,
    new_value,
    lengths,
    norm_gain,
    router_weight,
    expert_ids,
    w_gate,
    w_up,
    w_down,
):
    row_count = resid.shape[0]
    width_local = resid.shape[1]
    kv_local = key_cache.shape[1]
    cache_slots = key_cache.shape[2]
    head_size = key_cache.shape[3]
    group_size = query.shape[1] // (kv_local * head_size)
    expert_devices = lax.axis_size("expert")
    score_scale = 1.0 / math.sqrt(head_size)
    queries = query.reshape(row_count, kv_local, group_size, head_size)
    scores = (
        jnp.einsum("rkgd,rkld->rkgl", queries, key_cache, preferred_element_type=jnp.float32)
        * score_scale
    )
    fresh_score = (
        jnp.einsum(
            "rkgd,rkd->rkg",
            queries,
            new_key.reshape(row_count, kv_local, head_size),
            preferred_element_type=jnp.float32,
        )
        * score_scale
    )
    usable = lax.broadcasted_iota(jnp.int32, (row_count, cache_slots), 1) < lengths[:, None]
    powers = jnp.where(usable[:, None, None, :], jnp.exp(scores), jnp.float32(0.0))
    fresh_power = jnp.exp(fresh_score)
    denominator = jnp.sum(powers, axis=-1) + fresh_power
    weights_cache = (powers / denominator[..., None]).astype(jnp.bfloat16)
    weight_fresh = (fresh_power / denominator).astype(jnp.bfloat16)
    attended = jnp.einsum(
        "rkgl,rkld->rkgd", weights_cache, value_cache, preferred_element_type=jnp.float32
    )
    attended = attended + weight_fresh.astype(jnp.float32)[..., None] * new_value.astype(
        jnp.float32
    ).reshape(row_count, kv_local, 1, head_size)
    hidden_state = resid.astype(jnp.float32) + attended.reshape(row_count, width_local)

    gained = hidden_state * norm_gain
    sums = jnp.concatenate(
        [
            jnp.sum(hidden_state * hidden_state, axis=1, keepdims=True),
            jnp.dot(gained, router_weight, precision=lax.Precision.HIGHEST),
        ],
        axis=1,
    )
    pieces = split_three(sums)
    columns = sums.shape[1]
    payload = jnp.concatenate(
        [gained.astype(jnp.bfloat16)]
        + pieces
        + [jnp.zeros((row_count, 128 - 3 * columns), jnp.bfloat16)],
        axis=1,
    )
    gathered = lax.all_gather(payload, "expert", axis=0)
    whole_rows = gathered[:, :, :width_local]
    side = gathered[:, :, width_local:].astype(jnp.float32)
    sums = jnp.sum(
        side[:, :, :columns] + side[:, :, columns : 2 * columns] + side[:, :, 2 * columns : 3 * columns],
        axis=0,
    )
    scale = lax.rsqrt(sums[:, :1] / D + EPSILON)
    logits = sums[:, 1:] * scale

    choose = expert_ids[:, :, None] == lax.broadcasted_iota(jnp.int32, (1, 1, E), 2)
    picked = jnp.sum(jnp.where(choose, logits[:, None, :], jnp.float32(0.0)), axis=2)
    first_weight = 1.0 / (1.0 + jnp.exp(picked[:, 1] - picked[:, 0]))
    second_weight = 1.0 / (1.0 + jnp.exp(picked[:, 0] - picked[:, 1]))
    hits = jnp.sum(choose.astype(jnp.int32), axis=1)
    before = jnp.cumsum(hits, axis=0) - hits
    slot_index = jnp.sum(jnp.where(choose, before[:, None, :], 0), axis=2)
    own_expert = lax.axis_index("expert")
    own_slot = jnp.sum(jnp.where(expert_ids == own_expert, slot_index + 1, 0), axis=1) - 1
    own_selector = (
        lax.broadcasted_iota(jnp.int32, (CAP, row_count), 0) == own_slot[None, :]
    )
    outgoing = jnp.einsum(
        "cr,erd->ced",
        own_selector.astype(jnp.bfloat16),
        whole_rows,
        preferred_element_type=jnp.float32,
    ).reshape(CAP, D)
    own_scale = jnp.sum(
        jnp.where(own_selector, scale[:, 0][None, :], jnp.float32(0.0)), axis=1, keepdims=True
    )
    outgoing = (outgoing * own_scale).astype(jnp.bfloat16)

    near_up = shift_first(outgoing, 1)
    near_down = shift_first(outgoing, -1)
    far_low = shift_first(near_up[:HALF], 1)
    far_high = shift_first(near_down[HALF:], -1)
    line = jnp.concatenate([outgoing, near_up, near_down, far_low, far_high], axis=0)
    middle = line.shape[0] // 2
    line_up = shift_second(line, 1)
    line_down = shift_second(line, -1)
    line_far_low = shift_second(line_up[:middle], 1)
    line_far_high = shift_second(line_down[middle:], -1)

    part_own = feed([line], w_gate, w_up, w_down)
    part_near = feed([line_up, line_down], w_gate, w_up, w_down)
    part_far = feed([line_far_low, line_far_high], w_gate, w_up, w_down)

    line_sum = ring_sum(
        part_near[: 2 * middle],
        part_own,
        part_near[2 * middle :],
        part_far[:middle],
        part_far[middle:],
        shift_second,
    ).astype(jnp.bfloat16)
    expert_result = ring_sum(
        line_sum[CAP : 2 * CAP],
        line_sum[:CAP],
        line_sum[2 * CAP : 3 * CAP],
        line_sum[3 * CAP : 3 * CAP + HALF],
        line_sum[3 * CAP + HALF :],
        shift_first,
    ).astype(jnp.bfloat16)

    expert_result = expert_result.reshape(CAP, 1, expert_devices, width_local)
    returned = lax.all_to_all(expert_result, "expert", split_axis=2, concat_axis=1, tiled=True)
    flat_result = returned.reshape(CAP * E, width_local)
    target_index = slot_index * E + expert_ids
    picker = (
        target_index[:, :, None] == lax.broadcasted_iota(jnp.int32, (1, 1, CAP * E), 2)
    ).astype(jnp.bfloat16)
    taken = jnp.einsum("rkm,md->krd", picker, flat_result, preferred_element_type=jnp.float32)
    total = hidden_state + first_weight[:, None] * taken[0] + second_weight[:, None] * taken[1]
    return total.astype(jnp.bfloat16)


def solution(mesh):
    return jax.shard_map(
        on_device,
        mesh=mesh,
        in_specs=(
            P("attn", "expert"),
            P("attn", "expert"),
            P("attn", "expert", None, None),
            P("attn", "expert", None, None),
            P("attn", "expert"),
            P("attn", "expert"),
            P("attn"),
            P("expert"),
            P("expert", None),
            P("attn", None),
            P("expert", None, "attn"),
            P("expert", None, "attn"),
            P("expert", "attn", None),
        ),
        out_specs=P("attn", "expert"),
        check_vma=False,
    )
```

```python
import functools
import math

import jax
import jax.numpy as jnp
from jax import lax
from jax.experimental import pallas as pl
from jax.experimental.pallas import tpu as pltpu
from jax.sharding import PartitionSpec as P

D = 6144
E = 8
CAP = 32
SIDE = 4
CHAINS = 2
CHAIN_ROWS = CAP // CHAINS


EPSILON = 1e-05


def ring_pairs(step, second):
    pairs = []
    for z in range(SIDE):
        for x in range(SIDE):
            for y in range(SIDE):
                for core in range(2):
                    along_z = (core == 0) != second
                    to_z = (z + step) % SIDE if along_z else z
                    to_x = x if along_z else (x + step) % SIDE
                    source = (z * SIDE + x) * E + y * 2 + core
                    target = (to_z * SIDE + to_x) * E + y * 2 + core
                    pairs.append((source, target))
    return pairs


def shift_first(value, step):
    return lax.ppermute(value, ("attn", "expert"), ring_pairs(step, False))


def shift_second(value, step):
    return lax.ppermute(value, ("attn", "expert"), ring_pairs(step, True))


def split_three(value):
    high = value.astype(jnp.bfloat16)
    rest = value - high.astype(jnp.float32)
    middle = rest.astype(jnp.bfloat16)
    low = (rest - middle.astype(jnp.float32)).astype(jnp.bfloat16)
    return [high, middle, low]


def add_rounded(one, other):
    return (one.astype(jnp.float32) + other.astype(jnp.float32)).astype(jnp.bfloat16)


def ring_sum(behind, own, ahead, far_low, far_high, shift):
    half = far_low.shape[0]
    got_low = shift(far_low, 1)
    got_high = shift(far_high, -1)
    up = jnp.concatenate([add_rounded(ahead[:half], got_low), ahead[half:]], axis=0)
    down = jnp.concatenate([behind[:half], add_rounded(behind[half:], got_high)], axis=0)
    from_behind = shift(up, 1)
    from_ahead = shift(down, -1)
    return (
        own.astype(jnp.float32) + from_behind.astype(jnp.float32) + from_ahead.astype(jnp.float32)
    )


CHUNKS = 4


def feed_kernel(count, *refs):
    row_refs = refs[:count]
    gate_hbm, up_hbm, down_hbm, out_ref, rows, gate, up, down, ready = refs[count:]
    width, hidden = gate.shape
    depth = width // CHUNKS
    copies = []
    for k in range(CHUNKS):
        part = pl.ds(k * depth, depth)
        copies.append(
            pltpu.make_async_copy(gate_hbm.at[0, part, :], gate.at[part, :], ready.at[0, k])
        )
        copies.append(pltpu.make_async_copy(up_hbm.at[0, part, :], up.at[part, :], ready.at[1, k]))
    for k in range(CHUNKS):
        part = pl.ds(k * depth, depth)
        copies.append(
            pltpu.make_async_copy(down_hbm.at[0, :, part], down.at[:, part], ready.at[2, k])
        )
    for copy in copies:
        copy.start()
    at = 0
    for ref in row_refs:
        rows[at : at + ref.shape[0], :] = ref[...]
        at += ref.shape[0]
    gate_sum = jnp.zeros((rows.shape[0], hidden), jnp.float32)
    up_sum = jnp.zeros((rows.shape[0], hidden), jnp.float32)
    for k in range(CHUNKS):
        part = rows[:, k * depth : (k + 1) * depth]
        copies[2 * k].wait()
        gate_sum += jnp.dot(
            part, gate[k * depth : (k + 1) * depth, :], preferred_element_type=jnp.float32
        )
        copies[2 * k + 1].wait()
        up_sum += jnp.dot(
            part, up[k * depth : (k + 1) * depth, :], preferred_element_type=jnp.float32
        )
    active = (jax.nn.silu(gate_sum) * up_sum).astype(jnp.bfloat16)
    for k in range(CHUNKS):
        copies[2 * CHUNKS + k].wait()
        out_ref[:, k * depth : (k + 1) * depth] = jnp.dot(
            active, down[:, k * depth : (k + 1) * depth], preferred_element_type=jnp.float32
        ).astype(jnp.bfloat16)


def feed(row_arrays, w_gate, w_up, w_down):
    count = sum(array.shape[0] for array in row_arrays)
    width, hidden = w_gate.shape[1:]
    return pl.pallas_call(
        functools.partial(feed_kernel, len(row_arrays)),
        in_specs=[pl.BlockSpec(memory_space=pltpu.VMEM)] * len(row_arrays)
        + [pl.BlockSpec(memory_space=pltpu.HBM)] * 3,
        out_specs=pl.BlockSpec(memory_space=pltpu.VMEM),
        out_shape=jax.ShapeDtypeStruct((count, width), jnp.bfloat16),
        scratch_shapes=[
            pltpu.VMEM((count, width), jnp.bfloat16),
            pltpu.VMEM((width, hidden), jnp.bfloat16),
            pltpu.VMEM((width, hidden), jnp.bfloat16),
            pltpu.VMEM((hidden, width), jnp.bfloat16),
            pltpu.SemaphoreType.DMA((3, CHUNKS)),
        ],
        compiler_params=pltpu.CompilerParams(vmem_limit_bytes=46 * 1024 * 1024),
        cost_estimate=pl.CostEstimate(
            flops=6 * count * width * hidden,
            bytes_accessed=6 * width * hidden + 4 * count * width,
            transcendentals=count * hidden,
        ),
    )(*row_arrays, w_gate, w_up, w_down)


def gather_ring(block, shift):
    half = block.shape[0] // 2
    near_up = shift(block, 1)
    near_down = shift(block, -1)
    far_low = shift(near_up[:half], 1)
    far_high = shift(near_down[half:], -1)
    return block, near_up, near_down, far_low, far_high


def on_device(
    resid,
    query,
    key_cache,
    value_cache,
    new_key,
    new_value,
    lengths,
    norm_gain,
    router_weight,
    expert_ids,
    w_gate,
    w_up,
    w_down,
):
    row_count = resid.shape[0]
    width_local = resid.shape[1]
    kv_local = key_cache.shape[1]
    cache_slots = key_cache.shape[2]
    head_size = key_cache.shape[3]
    group_size = query.shape[1] // (kv_local * head_size)
    expert_devices = lax.axis_size("expert")
    score_scale = 1.0 / math.sqrt(head_size)
    queries = query.reshape(row_count, kv_local, group_size, head_size)
    scores = (
        jnp.einsum("rkgd,rkld->rkgl", queries, key_cache, preferred_element_type=jnp.float32)
        * score_scale
    )
    fresh_score = (
        jnp.einsum(
            "rkgd,rkd->rkg",
            queries,
            new_key.reshape(row_count, kv_local, head_size),
            preferred_element_type=jnp.float32,
        )
        * score_scale
    )
    usable = lax.broadcasted_iota(jnp.int32, (row_count, cache_slots), 1) < lengths[:, None]
    powers = jnp.where(usable[:, None, None, :], jnp.exp(scores), jnp.float32(0.0))
    fresh_power = jnp.exp(fresh_score)
    denominator = jnp.sum(powers, axis=-1) + fresh_power
    weights_cache = (powers / denominator[..., None]).astype(jnp.bfloat16)
    weight_fresh = (fresh_power / denominator).astype(jnp.bfloat16)
    attended = jnp.einsum(
        "rkgl,rkld->rkgd", weights_cache, value_cache, preferred_element_type=jnp.float32
    )
    attended = attended + weight_fresh.astype(jnp.float32)[..., None] * new_value.astype(
        jnp.float32
    ).reshape(row_count, kv_local, 1, head_size)
    hidden_state = resid.astype(jnp.float32) + attended.reshape(row_count, width_local)

    gained = hidden_state * norm_gain
    sums = jnp.concatenate(
        [
            jnp.sum(hidden_state * hidden_state, axis=1, keepdims=True),
            jnp.dot(gained, router_weight, precision=lax.Precision.HIGHEST),
        ],
        axis=1,
    )
    pieces = split_three(sums)
    columns = sums.shape[1]
    payload = jnp.concatenate(
        [gained.astype(jnp.bfloat16)]
        + pieces
        + [jnp.zeros((row_count, 128 - 3 * columns), jnp.bfloat16)],
        axis=1,
    )
    gathered = lax.all_gather(payload, "expert", axis=0)
    whole_rows = gathered[:, :, :width_local]
    side = gathered[:, :, width_local:].astype(jnp.float32)
    sums = jnp.sum(
        side[:, :, :columns] + side[:, :, columns : 2 * columns] + side[:, :, 2 * columns : 3 * columns],
        axis=0,
    )
    scale = lax.rsqrt(sums[:, :1] / D + EPSILON)
    logits = sums[:, 1:] * scale

    choose = expert_ids[:, :, None] == lax.broadcasted_iota(jnp.int32, (1, 1, E), 2)
    picked = jnp.sum(jnp.where(choose, logits[:, None, :], jnp.float32(0.0)), axis=2)
    first_weight = 1.0 / (1.0 + jnp.exp(picked[:, 1] - picked[:, 0]))
    second_weight = 1.0 / (1.0 + jnp.exp(picked[:, 0] - picked[:, 1]))
    hits = jnp.sum(choose.astype(jnp.int32), axis=1)
    before = jnp.cumsum(hits, axis=0) - hits
    slot_index = jnp.sum(jnp.where(choose, before[:, None, :], 0), axis=2)
    own_expert = lax.axis_index("expert")
    own_slot = jnp.sum(jnp.where(expert_ids == own_expert, slot_index + 1, 0), axis=1) - 1
    own_selector = (
        lax.broadcasted_iota(jnp.int32, (CAP, row_count), 0) == own_slot[None, :]
    )
    outgoing = jnp.einsum(
        "cr,erd->ced",
        own_selector.astype(jnp.bfloat16),
        whole_rows,
        preferred_element_type=jnp.float32,
    ).reshape(CAP, D)
    own_scale = jnp.sum(
        jnp.where(own_selector, scale[:, 0][None, :], jnp.float32(0.0)), axis=1, keepdims=True
    )
    outgoing = (outgoing * own_scale).astype(jnp.bfloat16)

    weights = (w_gate, w_up, w_down)
    lines = []
    for chain in range(CHAINS):
        slab = outgoing[chain * CHAIN_ROWS : (chain + 1) * CHAIN_ROWS]
        line = jnp.concatenate(gather_ring(slab, shift_first), axis=0)
        lines.append(gather_ring(line, shift_second))
    part_own = feed([line[0] for line in lines], *weights)
    part_near = [feed([line[1], line[2]], *weights) for line in lines]
    part_far = feed([piece for line in lines for piece in line[3:]], *weights)
    results = []
    for chain in range(CHAINS):
        count = SIDE * CHAIN_ROWS
        line_sum = ring_sum(
            part_near[chain][:count],
            part_own[chain * count : (chain + 1) * count],
            part_near[chain][count:],
            part_far[chain * count : chain * count + count // 2],
            part_far[chain * count + count // 2 : (chain + 1) * count],
            shift_second,
        ).astype(jnp.bfloat16)
        row = CHAIN_ROWS
        results.append(
            ring_sum(
                line_sum[row : 2 * row],
                line_sum[:row],
                line_sum[2 * row : 3 * row],
                line_sum[3 * row : 3 * row + row // 2],
                line_sum[3 * row + row // 2 :],
                shift_first,
            ).astype(jnp.bfloat16)
        )
    expert_result = jnp.concatenate(results, axis=0)

    expert_result = expert_result.reshape(CAP, 1, expert_devices, width_local)
    returned = lax.all_to_all(expert_result, "expert", split_axis=2, concat_axis=1, tiled=True)
    flat_result = returned.reshape(CAP * E, width_local)
    target_index = slot_index * E + expert_ids
    picker = (
        target_index[:, :, None] == lax.broadcasted_iota(jnp.int32, (1, 1, CAP * E), 2)
    ).astype(jnp.bfloat16)
    taken = jnp.einsum("rkm,md->krd", picker, flat_result, preferred_element_type=jnp.float32)
    total = hidden_state + first_weight[:, None] * taken[0] + second_weight[:, None] * taken[1]
    return total.astype(jnp.bfloat16)


def solution(mesh):
    return jax.shard_map(
        on_device,
        mesh=mesh,
        in_specs=(
            P("attn", "expert"),
            P("attn", "expert"),
            P("attn", "expert", None, None),
            P("attn", "expert", None, None),
            P("attn", "expert"),
            P("attn", "expert"),
            P("attn"),
            P("expert"),
            P("expert", None),
            P("attn", None),
            P("expert", None, "attn"),
            P("expert", None, "attn"),
            P("expert", "attn", None),
        ),
        out_specs=P("attn", "expert"),
        check_vma=False,
    )
```

```python
import functools
import math

import jax
import jax.numpy as jnp
from jax import lax
from jax.experimental import pallas as pl
from jax.experimental.pallas import tpu as pltpu
from jax.sharding import PartitionSpec as P

D = 6144
E = 8
CAP = 32
SIDE = 4


EPSILON = 1e-05


def ring_pairs(step, second):
    pairs = []
    for z in range(SIDE):
        for x in range(SIDE):
            for y in range(SIDE):
                for core in range(2):
                    along_z = (core == 0) != second
                    to_z = (z + step) % SIDE if along_z else z
                    to_x = x if along_z else (x + step) % SIDE
                    source = (z * SIDE + x) * E + y * 2 + core
                    target = (to_z * SIDE + to_x) * E + y * 2 + core
                    pairs.append((source, target))
    return pairs


def shift_first(value, step):
    return lax.ppermute(value, ("attn", "expert"), ring_pairs(step, False))


def shift_second(value, step):
    return lax.ppermute(value, ("attn", "expert"), ring_pairs(step, True))


def split_three(value):
    high = value.astype(jnp.bfloat16)
    rest = value - high.astype(jnp.float32)
    middle = rest.astype(jnp.bfloat16)
    low = (rest - middle.astype(jnp.float32)).astype(jnp.bfloat16)
    return [high, middle, low]


def add_rounded(one, other):
    return (one.astype(jnp.float32) + other.astype(jnp.float32)).astype(jnp.bfloat16)


CHUNKS = 4


def feed_kernel(count, *refs):
    row_refs = refs[:count]
    gate_hbm, up_hbm, down_hbm = refs[count : count + 3]
    out_refs = refs[count + 3 : 2 * count + 3]
    rows, gate, up, down, ready = refs[2 * count + 3 :]
    width, hidden = gate.shape
    depth = width // CHUNKS
    copies = []
    for k in range(CHUNKS):
        part = pl.ds(k * depth, depth)
        copies.append(
            pltpu.make_async_copy(gate_hbm.at[0, part, :], gate.at[part, :], ready.at[0, k])
        )
        copies.append(pltpu.make_async_copy(up_hbm.at[0, part, :], up.at[part, :], ready.at[1, k]))
    for k in range(CHUNKS):
        part = pl.ds(k * depth, depth)
        copies.append(
            pltpu.make_async_copy(down_hbm.at[0, :, part], down.at[:, part], ready.at[2, k])
        )
    for copy in copies:
        copy.start()
    at = 0
    for ref in row_refs:
        rows[at : at + ref.shape[0], :] = ref[...]
        at += ref.shape[0]
    gate_sum = jnp.zeros((rows.shape[0], hidden), jnp.float32)
    up_sum = jnp.zeros((rows.shape[0], hidden), jnp.float32)
    for k in range(CHUNKS):
        part = rows[:, k * depth : (k + 1) * depth]
        copies[2 * k].wait()
        gate_sum += jnp.dot(
            part, gate[k * depth : (k + 1) * depth, :], preferred_element_type=jnp.float32
        )
        copies[2 * k + 1].wait()
        up_sum += jnp.dot(
            part, up[k * depth : (k + 1) * depth, :], preferred_element_type=jnp.float32
        )
    active = (jax.nn.silu(gate_sum) * up_sum).astype(jnp.bfloat16)
    for k in range(CHUNKS):
        copies[2 * CHUNKS + k].wait()
        partial = jnp.dot(
            active, down[:, k * depth : (k + 1) * depth], preferred_element_type=jnp.float32
        ).astype(jnp.bfloat16)
        at = 0
        for ref in out_refs:
            ref[:, k * depth : (k + 1) * depth] = partial[at : at + ref.shape[0]]
            at += ref.shape[0]


def feed(row_arrays, w_gate, w_up, w_down):
    count = sum(array.shape[0] for array in row_arrays)
    width, hidden = w_gate.shape[1:]
    return pl.pallas_call(
        functools.partial(feed_kernel, len(row_arrays)),
        in_specs=[pl.BlockSpec(memory_space=pltpu.VMEM)] * len(row_arrays)
        + [pl.BlockSpec(memory_space=pltpu.HBM)] * 3,
        out_specs=[pl.BlockSpec(memory_space=pltpu.VMEM)] * len(row_arrays),
        out_shape=[jax.ShapeDtypeStruct(array.shape, jnp.bfloat16) for array in row_arrays],
        scratch_shapes=[
            pltpu.VMEM((count, width), jnp.bfloat16),
            pltpu.VMEM((width, hidden), jnp.bfloat16),
            pltpu.VMEM((width, hidden), jnp.bfloat16),
            pltpu.VMEM((hidden, width), jnp.bfloat16),
            pltpu.SemaphoreType.DMA((3, CHUNKS)),
        ],
        compiler_params=pltpu.CompilerParams(vmem_limit_bytes=46 * 1024 * 1024),
        cost_estimate=pl.CostEstimate(
            flops=6 * count * width * hidden,
            bytes_accessed=6 * width * hidden + 4 * count * width,
            transcendentals=count * hidden,
        ),
    )(*row_arrays, w_gate, w_up, w_down)


def spread_near(block, shift):
    return shift(block, 1), shift(block, -1)


def spread_far(near_up, near_down, shift):
    half = near_up.shape[0] // 2
    return shift(near_up[:half], 1), shift(near_down[half:], -1)


def halves_added(ahead, behind, far_low, far_high, shift):
    half = far_low.shape[0]
    got_low, got_high = shift(far_low, 1), shift(far_high, -1)
    up = ahead.at[:half].set(add_rounded(ahead[:half], got_low))
    down = behind.at[half:].set(add_rounded(behind[half:], got_high))
    return up, down


def add_three(own, one, other):
    total = own.astype(jnp.float32) + one.astype(jnp.float32) + other.astype(jnp.float32)
    return total.astype(jnp.bfloat16)


def on_device(
    resid,
    query,
    key_cache,
    value_cache,
    new_key,
    new_value,
    lengths,
    norm_gain,
    router_weight,
    expert_ids,
    w_gate,
    w_up,
    w_down,
):
    row_count = resid.shape[0]
    width_local = resid.shape[1]
    kv_local = key_cache.shape[1]
    cache_slots = key_cache.shape[2]
    head_size = key_cache.shape[3]
    group_size = query.shape[1] // (kv_local * head_size)
    expert_devices = lax.axis_size("expert")
    score_scale = 1.0 / math.sqrt(head_size)
    queries = query.reshape(row_count, kv_local, group_size, head_size)
    scores = (
        jnp.einsum("rkgd,rkld->rkgl", queries, key_cache, preferred_element_type=jnp.float32)
        * score_scale
    )
    fresh_score = (
        jnp.einsum(
            "rkgd,rkd->rkg",
            queries,
            new_key.reshape(row_count, kv_local, head_size),
            preferred_element_type=jnp.float32,
        )
        * score_scale
    )
    usable = lax.broadcasted_iota(jnp.int32, (row_count, cache_slots), 1) < lengths[:, None]
    powers = jnp.where(usable[:, None, None, :], jnp.exp(scores), jnp.float32(0.0))
    fresh_power = jnp.exp(fresh_score)
    denominator = jnp.sum(powers, axis=-1) + fresh_power
    weights_cache = (powers / denominator[..., None]).astype(jnp.bfloat16)
    weight_fresh = (fresh_power / denominator).astype(jnp.bfloat16)
    attended = jnp.einsum(
        "rkgl,rkld->rkgd", weights_cache, value_cache, preferred_element_type=jnp.float32
    )
    attended = attended + weight_fresh.astype(jnp.float32)[..., None] * new_value.astype(
        jnp.float32
    ).reshape(row_count, kv_local, 1, head_size)
    hidden_state = resid.astype(jnp.float32) + attended.reshape(row_count, width_local)

    gained = hidden_state * norm_gain
    sums = jnp.concatenate(
        [
            jnp.sum(hidden_state * hidden_state, axis=1, keepdims=True),
            jnp.dot(gained, router_weight, precision=lax.Precision.HIGHEST),
        ],
        axis=1,
    )
    pieces = split_three(sums)
    columns = sums.shape[1]
    payload = jnp.concatenate(
        [gained.astype(jnp.bfloat16)]
        + pieces
        + [jnp.zeros((row_count, 128 - 3 * columns), jnp.bfloat16)],
        axis=1,
    )
    gathered = lax.all_gather(payload, "expert", axis=0)
    whole_rows = gathered[:, :, :width_local]
    side = gathered[:, :, width_local:].astype(jnp.float32)
    sums = jnp.sum(
        side[:, :, :columns] + side[:, :, columns : 2 * columns] + side[:, :, 2 * columns : 3 * columns],
        axis=0,
    )
    scale = lax.rsqrt(sums[:, :1] / D + EPSILON)
    logits = sums[:, 1:] * scale

    choose = expert_ids[:, :, None] == lax.broadcasted_iota(jnp.int32, (1, 1, E), 2)
    picked = jnp.sum(jnp.where(choose, logits[:, None, :], jnp.float32(0.0)), axis=2)
    first_weight = 1.0 / (1.0 + jnp.exp(picked[:, 1] - picked[:, 0]))
    second_weight = 1.0 / (1.0 + jnp.exp(picked[:, 0] - picked[:, 1]))
    hits = jnp.sum(choose.astype(jnp.int32), axis=1)
    before = jnp.cumsum(hits, axis=0) - hits
    slot_index = jnp.sum(jnp.where(choose, before[:, None, :], 0), axis=2)
    own_expert = lax.axis_index("expert")
    own_slot = jnp.sum(jnp.where(expert_ids == own_expert, slot_index + 1, 0), axis=1) - 1
    own_selector = (
        lax.broadcasted_iota(jnp.int32, (CAP, row_count), 0) == own_slot[None, :]
    )
    outgoing = jnp.einsum(
        "cr,erd->ced",
        own_selector.astype(jnp.bfloat16),
        whole_rows,
        preferred_element_type=jnp.float32,
    ).reshape(CAP, D)
    own_scale = jnp.sum(
        jnp.where(own_selector, scale[:, 0][None, :], jnp.float32(0.0)), axis=1, keepdims=True
    )
    outgoing = (outgoing * own_scale).astype(jnp.bfloat16)

    weights = (w_gate, w_up, w_down)
    near_up, near_down = spread_near(outgoing, shift_first)
    far_low, far_high = spread_far(near_up, near_down, shift_first)
    one = jnp.concatenate([outgoing, near_up], axis=0)
    two = jnp.concatenate([near_down, far_low, far_high], axis=0)
    one_near = spread_near(one, shift_second)
    two_near = spread_near(two, shift_second)
    one_far = spread_far(*one_near, shift_second)
    one_near_part = feed(one_near, *weights)
    two_near, one_near_part = lax.optimization_barrier((two_near, one_near_part))
    two_far = spread_far(*two_near, shift_second)
    two_near_part = feed(two_near, *weights)
    two_far, two_near_part = lax.optimization_barrier((two_far, two_near_part))
    far_part = feed([*one_far, *two_far], *weights)

    two_up, two_down = halves_added(
        two_near_part[1], two_near_part[0], far_part[2], far_part[3], shift_second
    )
    one_up, one_down = halves_added(
        one_near_part[1], one_near_part[0], far_part[0], far_part[1], shift_second
    )
    one, two = lax.optimization_barrier((one, two, one_up, one_down, two_up, two_down))[:2]
    one_own, two_own = feed([one, two], *weights)
    two_sum = add_three(two_own, shift_second(two_up, 1), shift_second(two_down, -1))
    one_sum = add_three(one_own, shift_second(one_up, 1), shift_second(one_down, -1))
    up, down = halves_added(
        two_sum[:CAP],
        one_sum[CAP:],
        two_sum[CAP : CAP + CAP // 2],
        two_sum[CAP + CAP // 2 :],
        shift_first,
    )
    expert_result = add_three(one_sum[:CAP], shift_first(up, 1), shift_first(down, -1))

    expert_result = expert_result.reshape(CAP, 1, expert_devices, width_local)
    returned = lax.all_to_all(expert_result, "expert", split_axis=2, concat_axis=1, tiled=True)
    flat_result = returned.reshape(CAP * E, width_local)
    target_index = slot_index * E + expert_ids
    picker = (
        target_index[:, :, None] == lax.broadcasted_iota(jnp.int32, (1, 1, CAP * E), 2)
    ).astype(jnp.bfloat16)
    taken = jnp.einsum("rkm,md->krd", picker, flat_result, preferred_element_type=jnp.float32)
    total = hidden_state + first_weight[:, None] * taken[0] + second_weight[:, None] * taken[1]
    return total.astype(jnp.bfloat16)


def solution(mesh):
    return jax.shard_map(
        on_device,
        mesh=mesh,
        in_specs=(
            P("attn", "expert"),
            P("attn", "expert"),
            P("attn", "expert", None, None),
            P("attn", "expert", None, None),
            P("attn", "expert"),
            P("attn", "expert"),
            P("attn"),
            P("expert"),
            P("expert", None),
            P("attn", None),
            P("expert", None, "attn"),
            P("expert", None, "attn"),
            P("expert", "attn", None),
        ),
        out_specs=P("attn", "expert"),
        check_vma=False,
    )
```

```python
import functools
import math

import jax
import jax.numpy as jnp
from jax import lax
from jax.experimental import pallas as pl
from jax.experimental.pallas import tpu as pltpu
from jax.sharding import PartitionSpec as P

D = 6144
E = 8
CAP = 32
SIDE = 4


EPSILON = 1e-05


def ring_pairs(step, second):
    pairs = []
    for z in range(SIDE):
        for x in range(SIDE):
            for y in range(SIDE):
                for core in range(2):
                    along_z = (core == 0) != second
                    to_z = (z + step) % SIDE if along_z else z
                    to_x = x if along_z else (x + step) % SIDE
                    source = (z * SIDE + x) * E + y * 2 + core
                    target = (to_z * SIDE + to_x) * E + y * 2 + core
                    pairs.append((source, target))
    return pairs


def shift_first(value, step):
    return lax.ppermute(value, ("attn", "expert"), ring_pairs(step, False))


def shift_second(value, step):
    return lax.ppermute(value, ("attn", "expert"), ring_pairs(step, True))


def split_three(value):
    high = value.astype(jnp.bfloat16)
    rest = value - high.astype(jnp.float32)
    middle = rest.astype(jnp.bfloat16)
    low = (rest - middle.astype(jnp.float32)).astype(jnp.bfloat16)
    return [high, middle, low]


def add_rounded(one, other):
    return (one.astype(jnp.float32) + other.astype(jnp.float32)).astype(jnp.bfloat16)


CHUNKS = 4
LOAD_VMEM = 24 * 1024 * 1024
FEED_VMEM = 28 * 1024 * 1024


def load_kernel(*refs):
    sources, targets, ready = refs[:3], refs[3:6], refs[6]
    copies = []
    for index, (source, target) in enumerate(zip(sources, targets)):
        part = source.shape[1] // CHUNKS
        for k in range(CHUNKS):
            where = pl.ds(k * part, part)
            copies.append(
                pltpu.make_async_copy(
                    source.at[:, where, :], target.at[:, where, :], ready.at[index, k]
                )
            )
    for copy in copies:
        copy.start()
    for copy in copies:
        copy.wait()


def load(*arrays):
    size = sum(array.size * 2 for array in arrays)
    return pl.pallas_call(
        load_kernel,
        in_specs=[pl.BlockSpec(memory_space=pltpu.HBM)] * 3,
        out_specs=[pl.BlockSpec(memory_space=pltpu.VMEM)] * 3,
        out_shape=[jax.ShapeDtypeStruct(array.shape, array.dtype) for array in arrays],
        scratch_shapes=[pltpu.SemaphoreType.DMA((3, CHUNKS))],
        compiler_params=pltpu.CompilerParams(vmem_limit_bytes=LOAD_VMEM),
        cost_estimate=pl.CostEstimate(flops=0, bytes_accessed=size, transcendentals=0),
    )(*arrays)


def feed_kernel(count, *refs):
    row_refs = refs[:count]
    gate, up, down = refs[count : count + 3]
    out_refs = refs[count + 3 : 2 * count + 3]
    rows = refs[-1]
    width, hidden = gate.shape[1:]
    depth = width // CHUNKS
    at = 0
    for ref in row_refs:
        rows[at : at + ref.shape[0], :] = ref[...]
        at += ref.shape[0]
    gate_sum = jnp.zeros((rows.shape[0], hidden), jnp.float32)
    up_sum = jnp.zeros((rows.shape[0], hidden), jnp.float32)
    for k in range(CHUNKS):
        part = rows[:, k * depth : (k + 1) * depth]
        gate_sum += jnp.dot(
            part, gate[0, k * depth : (k + 1) * depth, :], preferred_element_type=jnp.float32
        )
        up_sum += jnp.dot(
            part, up[0, k * depth : (k + 1) * depth, :], preferred_element_type=jnp.float32
        )
    active = (jax.nn.silu(gate_sum) * up_sum).astype(jnp.bfloat16)
    for k in range(CHUNKS):
        partial = jnp.dot(
            active, down[0, :, k * depth : (k + 1) * depth], preferred_element_type=jnp.float32
        ).astype(jnp.bfloat16)
        at = 0
        for ref in out_refs:
            ref[:, k * depth : (k + 1) * depth] = partial[at : at + ref.shape[0]]
            at += ref.shape[0]


def feed(row_arrays, w_gate, w_up, w_down):
    count = sum(array.shape[0] for array in row_arrays)
    width, hidden = w_gate.shape[1:]
    return pl.pallas_call(
        functools.partial(feed_kernel, len(row_arrays)),
        in_specs=[pl.BlockSpec(memory_space=pltpu.VMEM)] * (len(row_arrays) + 3),
        out_specs=[pl.BlockSpec(memory_space=pltpu.VMEM)] * len(row_arrays),
        out_shape=[jax.ShapeDtypeStruct(array.shape, jnp.bfloat16) for array in row_arrays],
        scratch_shapes=[pltpu.VMEM((count, width), jnp.bfloat16)],
        compiler_params=pltpu.CompilerParams(vmem_limit_bytes=FEED_VMEM),
        cost_estimate=pl.CostEstimate(
            flops=6 * count * width * hidden,
            bytes_accessed=4 * count * width,
            transcendentals=count * hidden,
        ),
    )(*row_arrays, w_gate, w_up, w_down)


def spread_near(block, shift):
    return shift(block, 1), shift(block, -1)


def spread_far(near_up, near_down, shift):
    half = near_up.shape[0] // 2
    return shift(near_up[:half], 1), shift(near_down[half:], -1)


def halves_added(ahead, behind, far_low, far_high, shift):
    half = far_low.shape[0]
    got_low, got_high = shift(far_low, 1), shift(far_high, -1)
    up = ahead.at[:half].set(add_rounded(ahead[:half], got_low))
    down = behind.at[half:].set(add_rounded(behind[half:], got_high))
    return up, down


def add_three(own, one, other):
    total = own.astype(jnp.float32) + one.astype(jnp.float32) + other.astype(jnp.float32)
    return total.astype(jnp.bfloat16)


def on_device(
    resid,
    query,
    key_cache,
    value_cache,
    new_key,
    new_value,
    lengths,
    norm_gain,
    router_weight,
    expert_ids,
    w_gate,
    w_up,
    w_down,
):
    row_count = resid.shape[0]
    width_local = resid.shape[1]
    kv_local = key_cache.shape[1]
    cache_slots = key_cache.shape[2]
    head_size = key_cache.shape[3]
    group_size = query.shape[1] // (kv_local * head_size)
    expert_devices = lax.axis_size("expert")
    score_scale = 1.0 / math.sqrt(head_size)
    queries = query.reshape(row_count, kv_local, group_size, head_size)
    scores = (
        jnp.einsum("rkgd,rkld->rkgl", queries, key_cache, preferred_element_type=jnp.float32)
        * score_scale
    )
    fresh_score = (
        jnp.einsum(
            "rkgd,rkd->rkg",
            queries,
            new_key.reshape(row_count, kv_local, head_size),
            preferred_element_type=jnp.float32,
        )
        * score_scale
    )
    usable = lax.broadcasted_iota(jnp.int32, (row_count, cache_slots), 1) < lengths[:, None]
    powers = jnp.where(usable[:, None, None, :], jnp.exp(scores), jnp.float32(0.0))
    fresh_power = jnp.exp(fresh_score)
    denominator = jnp.sum(powers, axis=-1) + fresh_power
    weights_cache = (powers / denominator[..., None]).astype(jnp.bfloat16)
    weight_fresh = (fresh_power / denominator).astype(jnp.bfloat16)
    attended = jnp.einsum(
        "rkgl,rkld->rkgd", weights_cache, value_cache, preferred_element_type=jnp.float32
    )
    attended = attended + weight_fresh.astype(jnp.float32)[..., None] * new_value.astype(
        jnp.float32
    ).reshape(row_count, kv_local, 1, head_size)
    hidden_state = resid.astype(jnp.float32) + attended.reshape(row_count, width_local)

    gained = hidden_state * norm_gain
    sums = jnp.concatenate(
        [
            jnp.sum(hidden_state * hidden_state, axis=1, keepdims=True),
            jnp.dot(gained, router_weight, precision=lax.Precision.HIGHEST),
        ],
        axis=1,
    )
    pieces = split_three(sums)
    columns = sums.shape[1]
    payload = jnp.concatenate(
        [gained.astype(jnp.bfloat16)]
        + pieces
        + [jnp.zeros((row_count, 128 - 3 * columns), jnp.bfloat16)],
        axis=1,
    )
    gathered = lax.all_gather(payload, "expert", axis=0)
    whole_rows = gathered[:, :, :width_local]
    side = gathered[:, :, width_local:].astype(jnp.float32)
    sums = jnp.sum(
        side[:, :, :columns] + side[:, :, columns : 2 * columns] + side[:, :, 2 * columns : 3 * columns],
        axis=0,
    )
    scale = lax.rsqrt(sums[:, :1] / D + EPSILON)
    logits = sums[:, 1:] * scale

    choose = expert_ids[:, :, None] == lax.broadcasted_iota(jnp.int32, (1, 1, E), 2)
    picked = jnp.sum(jnp.where(choose, logits[:, None, :], jnp.float32(0.0)), axis=2)
    first_weight = 1.0 / (1.0 + jnp.exp(picked[:, 1] - picked[:, 0]))
    second_weight = 1.0 / (1.0 + jnp.exp(picked[:, 0] - picked[:, 1]))
    hits = jnp.sum(choose.astype(jnp.int32), axis=1)
    before = jnp.cumsum(hits, axis=0) - hits
    slot_index = jnp.sum(jnp.where(choose, before[:, None, :], 0), axis=2)
    own_expert = lax.axis_index("expert")
    own_slot = jnp.sum(jnp.where(expert_ids == own_expert, slot_index + 1, 0), axis=1) - 1
    own_selector = (
        lax.broadcasted_iota(jnp.int32, (CAP, row_count), 0) == own_slot[None, :]
    )
    outgoing = jnp.einsum(
        "cr,erd->ced",
        own_selector.astype(jnp.bfloat16),
        whole_rows,
        preferred_element_type=jnp.float32,
    ).reshape(CAP, D)
    own_scale = jnp.sum(
        jnp.where(own_selector, scale[:, 0][None, :], jnp.float32(0.0)), axis=1, keepdims=True
    )
    outgoing = (outgoing * own_scale).astype(jnp.bfloat16)

    near_up, near_down = spread_near(outgoing, shift_first)
    weights = load(w_gate, w_up, w_down)
    near_up, near_down, weights = lax.optimization_barrier((near_up, near_down, weights))
    far_low, far_high = spread_far(near_up, near_down, shift_first)
    outgoing, far_low, far_high = lax.optimization_barrier((outgoing, far_low, far_high))
    one = jnp.concatenate([outgoing, near_up], axis=0)
    two = jnp.concatenate([near_down, far_low, far_high], axis=0)
    one_near = spread_near(one, shift_second)
    two_near = spread_near(two, shift_second)
    one_far = spread_far(*one_near, shift_second)
    one_near_part = feed(one_near, *weights)
    two_near, one_near_part = lax.optimization_barrier((two_near, one_near_part))
    two_far = spread_far(*two_near, shift_second)
    two_near, one_far = lax.optimization_barrier((two_near, one_far))
    two_near_part = feed(two_near, *weights)
    two_far, two_near_part = lax.optimization_barrier((two_far, two_near_part))
    far_part = feed([*one_far, *two_far], *weights)

    two_up, two_down = halves_added(
        two_near_part[1], two_near_part[0], far_part[2], far_part[3], shift_second
    )
    one_up, one_down = halves_added(
        one_near_part[1], one_near_part[0], far_part[0], far_part[1], shift_second
    )
    one, two = lax.optimization_barrier((one, two, one_up, one_down, two_up, two_down))[:2]
    one_own, two_own = feed([one, two], *weights)
    two_sum = add_three(two_own, shift_second(two_up, 1), shift_second(two_down, -1))
    one_sum = add_three(one_own, shift_second(one_up, 1), shift_second(one_down, -1))
    up, down = halves_added(
        two_sum[:CAP],
        one_sum[CAP:],
        two_sum[CAP : CAP + CAP // 2],
        two_sum[CAP + CAP // 2 :],
        shift_first,
    )
    expert_result = add_three(one_sum[:CAP], shift_first(up, 1), shift_first(down, -1))

    expert_result = expert_result.reshape(CAP, 1, expert_devices, width_local)
    returned = lax.all_to_all(expert_result, "expert", split_axis=2, concat_axis=1, tiled=True)
    flat_result = returned.reshape(CAP * E, width_local)
    target_index = slot_index * E + expert_ids
    picker = (
        target_index[:, :, None] == lax.broadcasted_iota(jnp.int32, (1, 1, CAP * E), 2)
    ).astype(jnp.bfloat16)
    taken = jnp.einsum("rkm,md->krd", picker, flat_result, preferred_element_type=jnp.float32)
    total = hidden_state + first_weight[:, None] * taken[0] + second_weight[:, None] * taken[1]
    return total.astype(jnp.bfloat16)


def solution(mesh):
    return jax.shard_map(
        on_device,
        mesh=mesh,
        in_specs=(
            P("attn", "expert"),
            P("attn", "expert"),
            P("attn", "expert", None, None),
            P("attn", "expert", None, None),
            P("attn", "expert"),
            P("attn", "expert"),
            P("attn"),
            P("expert"),
            P("expert", None),
            P("attn", None),
            P("expert", None, "attn"),
            P("expert", None, "attn"),
            P("expert", "attn", None),
        ),
        out_specs=P("attn", "expert"),
        check_vma=False,
    )
```

```python
import functools
import math

import jax
import jax.numpy as jnp
from jax import lax
from jax.experimental import pallas as pl
from jax.experimental.pallas import tpu as pltpu
from jax.sharding import PartitionSpec as P

D = 6144
E = 8
CAP = 32
SIDE = 4


EPSILON = 1e-05
CHAINS = 2
CHAIN_ROWS = CAP // CHAINS


def ring_pairs(step, second):
    pairs = []
    for z in range(SIDE):
        for x in range(SIDE):
            for y in range(SIDE):
                for core in range(2):
                    along_z = (core == 0) != second
                    to_z = (z + step) % SIDE if along_z else z
                    to_x = x if along_z else (x + step) % SIDE
                    source = (z * SIDE + x) * E + y * 2 + core
                    target = (to_z * SIDE + to_x) * E + y * 2 + core
                    pairs.append((source, target))
    return pairs


def shift_first(value, step):
    return lax.ppermute(value, ("attn", "expert"), ring_pairs(step, False))


def shift_second(value, step):
    return lax.ppermute(value, ("attn", "expert"), ring_pairs(step, True))


def split_three(value):
    high = value.astype(jnp.bfloat16)
    rest = value - high.astype(jnp.float32)
    middle = rest.astype(jnp.bfloat16)
    low = (rest - middle.astype(jnp.float32)).astype(jnp.bfloat16)
    return [high, middle, low]


def add_rounded(one, other):
    return (one.astype(jnp.float32) + other.astype(jnp.float32)).astype(jnp.bfloat16)


CHUNKS = 4
LOAD_VMEM = 24 * 1024 * 1024
FEED_VMEM = 16 * 1024 * 1024


def load_kernel(*refs):
    sources, targets, ready = refs[:3], refs[3:6], refs[6]
    copies = []
    for index, (source, target) in enumerate(zip(sources, targets)):
        part = source.shape[1] // CHUNKS
        for k in range(CHUNKS):
            where = pl.ds(k * part, part)
            copies.append(
                pltpu.make_async_copy(
                    source.at[:, where, :], target.at[:, where, :], ready.at[index, k]
                )
            )
    for copy in copies:
        copy.start()
    for copy in copies:
        copy.wait()


def load(*arrays):
    size = sum(array.size * 2 for array in arrays)
    return pl.pallas_call(
        load_kernel,
        in_specs=[pl.BlockSpec(memory_space=pltpu.HBM)] * 3,
        out_specs=[pl.BlockSpec(memory_space=pltpu.VMEM)] * 3,
        out_shape=[jax.ShapeDtypeStruct(array.shape, array.dtype) for array in arrays],
        scratch_shapes=[pltpu.SemaphoreType.DMA((3, CHUNKS))],
        compiler_params=pltpu.CompilerParams(vmem_limit_bytes=LOAD_VMEM),
        cost_estimate=pl.CostEstimate(flops=0, bytes_accessed=size, transcendentals=0),
    )(*arrays)


def feed_kernel(count, *refs):
    row_refs = refs[:count]
    gate, up, down = refs[count : count + 3]
    out_refs = refs[count + 3 : 2 * count + 3]
    rows = refs[-1]
    width, hidden = gate.shape[1:]
    depth = width // CHUNKS
    at = 0
    for ref in row_refs:
        rows[at : at + ref.shape[0], :] = ref[...]
        at += ref.shape[0]
    gate_sum = jnp.zeros((rows.shape[0], hidden), jnp.float32)
    up_sum = jnp.zeros((rows.shape[0], hidden), jnp.float32)
    for k in range(CHUNKS):
        part = rows[:, k * depth : (k + 1) * depth]
        gate_sum += jnp.dot(
            part, gate[0, k * depth : (k + 1) * depth, :], preferred_element_type=jnp.float32
        )
        up_sum += jnp.dot(
            part, up[0, k * depth : (k + 1) * depth, :], preferred_element_type=jnp.float32
        )
    active = (jax.nn.silu(gate_sum) * up_sum).astype(jnp.bfloat16)
    for k in range(CHUNKS):
        partial = jnp.dot(
            active, down[0, :, k * depth : (k + 1) * depth], preferred_element_type=jnp.float32
        ).astype(jnp.bfloat16)
        at = 0
        for ref in out_refs:
            ref[:, k * depth : (k + 1) * depth] = partial[at : at + ref.shape[0]]
            at += ref.shape[0]


def feed(row_arrays, w_gate, w_up, w_down):
    count = sum(array.shape[0] for array in row_arrays)
    width, hidden = w_gate.shape[1:]
    return pl.pallas_call(
        functools.partial(feed_kernel, len(row_arrays)),
        in_specs=[pl.BlockSpec(memory_space=pltpu.VMEM)] * (len(row_arrays) + 3),
        out_specs=[pl.BlockSpec(memory_space=pltpu.VMEM)] * len(row_arrays),
        out_shape=[jax.ShapeDtypeStruct(array.shape, jnp.bfloat16) for array in row_arrays],
        scratch_shapes=[pltpu.VMEM((count, width), jnp.bfloat16)],
        compiler_params=pltpu.CompilerParams(vmem_limit_bytes=FEED_VMEM),
        cost_estimate=pl.CostEstimate(
            flops=6 * count * width * hidden,
            bytes_accessed=4 * count * width,
            transcendentals=count * hidden,
        ),
    )(*row_arrays, w_gate, w_up, w_down)


def spread_near(block, shift):
    return shift(block, 1), shift(block, -1)


def spread_far(near_up, near_down, shift):
    half = near_up.shape[0] // 2
    return shift(near_up[:half], 1), shift(near_down[half:], -1)


def halves_added(ahead, behind, far_low, far_high, shift):
    half = far_low.shape[0]
    got_low, got_high = shift(far_low, 1), shift(far_high, -1)
    up = ahead.at[:half].set(add_rounded(ahead[:half], got_low))
    down = behind.at[half:].set(add_rounded(behind[half:], got_high))
    return up, down


def add_three(own, one, other):
    total = own.astype(jnp.float32) + one.astype(jnp.float32) + other.astype(jnp.float32)
    return total.astype(jnp.bfloat16)


def on_device(
    resid,
    query,
    key_cache,
    value_cache,
    new_key,
    new_value,
    lengths,
    norm_gain,
    router_weight,
    expert_ids,
    w_gate,
    w_up,
    w_down,
):
    row_count = resid.shape[0]
    width_local = resid.shape[1]
    kv_local = key_cache.shape[1]
    cache_slots = key_cache.shape[2]
    head_size = key_cache.shape[3]
    group_size = query.shape[1] // (kv_local * head_size)
    expert_devices = lax.axis_size("expert")
    score_scale = 1.0 / math.sqrt(head_size)
    queries = query.reshape(row_count, kv_local, group_size, head_size)
    scores = (
        jnp.einsum("rkgd,rkld->rkgl", queries, key_cache, preferred_element_type=jnp.float32)
        * score_scale
    )
    fresh_score = (
        jnp.einsum(
            "rkgd,rkd->rkg",
            queries,
            new_key.reshape(row_count, kv_local, head_size),
            preferred_element_type=jnp.float32,
        )
        * score_scale
    )
    usable = lax.broadcasted_iota(jnp.int32, (row_count, cache_slots), 1) < lengths[:, None]
    powers = jnp.where(usable[:, None, None, :], jnp.exp(scores), jnp.float32(0.0))
    fresh_power = jnp.exp(fresh_score)
    denominator = jnp.sum(powers, axis=-1) + fresh_power
    weights_cache = (powers / denominator[..., None]).astype(jnp.bfloat16)
    weight_fresh = (fresh_power / denominator).astype(jnp.bfloat16)
    attended = jnp.einsum(
        "rkgl,rkld->rkgd", weights_cache, value_cache, preferred_element_type=jnp.float32
    )
    attended = attended + weight_fresh.astype(jnp.float32)[..., None] * new_value.astype(
        jnp.float32
    ).reshape(row_count, kv_local, 1, head_size)
    hidden_state = resid.astype(jnp.float32) + attended.reshape(row_count, width_local)

    gained = hidden_state * norm_gain
    sums = jnp.concatenate(
        [
            jnp.sum(hidden_state * hidden_state, axis=1, keepdims=True),
            jnp.dot(gained, router_weight, precision=lax.Precision.HIGHEST),
        ],
        axis=1,
    )
    pieces = split_three(sums)
    columns = sums.shape[1]
    payload = jnp.concatenate(
        [gained.astype(jnp.bfloat16)]
        + pieces
        + [jnp.zeros((row_count, 128 - 3 * columns), jnp.bfloat16)],
        axis=1,
    )
    gathered = lax.all_gather(payload, "expert", axis=0)
    whole_rows = gathered[:, :, :width_local]
    side = gathered[:, :, width_local:].astype(jnp.float32)
    sums = jnp.sum(
        side[:, :, :columns] + side[:, :, columns : 2 * columns] + side[:, :, 2 * columns : 3 * columns],
        axis=0,
    )
    scale = lax.rsqrt(sums[:, :1] / D + EPSILON)
    logits = sums[:, 1:] * scale

    choose = expert_ids[:, :, None] == lax.broadcasted_iota(jnp.int32, (1, 1, E), 2)
    picked = jnp.sum(jnp.where(choose, logits[:, None, :], jnp.float32(0.0)), axis=2)
    first_weight = 1.0 / (1.0 + jnp.exp(picked[:, 1] - picked[:, 0]))
    second_weight = 1.0 / (1.0 + jnp.exp(picked[:, 0] - picked[:, 1]))
    hits = jnp.sum(choose.astype(jnp.int32), axis=1)
    before = jnp.cumsum(hits, axis=0) - hits
    slot_index = jnp.sum(jnp.where(choose, before[:, None, :], 0), axis=2)
    own_expert = lax.axis_index("expert")
    own_slot = jnp.sum(jnp.where(expert_ids == own_expert, slot_index + 1, 0), axis=1) - 1
    own_selector = (
        lax.broadcasted_iota(jnp.int32, (CAP, row_count), 0) == own_slot[None, :]
    )
    outgoing = jnp.einsum(
        "cr,erd->ced",
        own_selector.astype(jnp.bfloat16),
        whole_rows,
        preferred_element_type=jnp.float32,
    ).reshape(CAP, D)
    own_scale = jnp.sum(
        jnp.where(own_selector, scale[:, 0][None, :], jnp.float32(0.0)), axis=1, keepdims=True
    )
    outgoing = (outgoing * own_scale).astype(jnp.bfloat16)

    lines = []
    for chain in range(CHAINS):
        slab = outgoing[chain * CHAIN_ROWS : (chain + 1) * CHAIN_ROWS]
        near = spread_near(slab, shift_first)
        lines.append(jnp.concatenate([slab, *near, *spread_far(*near, shift_first)], axis=0))
    weights = lax.optimization_barrier((w_gate, w_up, w_down, *lines))[:3]
    weights = load(*weights)
    own_parts = feed(lines, *weights)
    nears = [spread_near(line, shift_second) for line in lines]
    nears[0], own_parts = lax.optimization_barrier((nears[0], own_parts))
    first_part = feed(nears[0], *weights)
    nears[1], first_part = lax.optimization_barrier((nears[1], first_part))
    fars = [spread_far(*near, shift_second) for near in nears]
    nears[1], fars[0] = lax.optimization_barrier((nears[1], fars[0]))
    near_parts = [first_part, feed(nears[1], *weights)]
    fars, near_parts = lax.optimization_barrier((fars, near_parts))
    far_part = feed([piece for far in fars for piece in far], *weights)

    results = []
    for chain in range(CHAINS):
        behind, ahead = near_parts[chain]
        far = far_part[2 * chain : 2 * chain + 2]
        up, down = halves_added(ahead, behind, *far, shift_second)
        line_sum = add_three(own_parts[chain], shift_second(up, 1), shift_second(down, -1))
        behind = line_sum[CHAIN_ROWS : 2 * CHAIN_ROWS]
        ahead = line_sum[2 * CHAIN_ROWS : 3 * CHAIN_ROWS]
        middle = 3 * CHAIN_ROWS + CHAIN_ROWS // 2
        far_low, far_high = line_sum[3 * CHAIN_ROWS : middle], line_sum[middle:]
        up, down = halves_added(ahead, behind, far_low, far_high, shift_first)
        results.append(
            add_three(line_sum[:CHAIN_ROWS], shift_first(up, 1), shift_first(down, -1))
        )
    expert_result = jnp.concatenate(results, axis=0)

    expert_result = expert_result.reshape(CAP, 1, expert_devices, width_local)
    returned = lax.all_to_all(expert_result, "expert", split_axis=2, concat_axis=1, tiled=True)
    flat_result = returned.reshape(CAP * E, width_local)
    target_index = slot_index * E + expert_ids
    picker = (
        target_index[:, :, None] == lax.broadcasted_iota(jnp.int32, (1, 1, CAP * E), 2)
    ).astype(jnp.bfloat16)
    taken = jnp.einsum("rkm,md->krd", picker, flat_result, preferred_element_type=jnp.float32)
    total = hidden_state + first_weight[:, None] * taken[0] + second_weight[:, None] * taken[1]
    return total.astype(jnp.bfloat16)


def solution(mesh):
    return jax.shard_map(
        on_device,
        mesh=mesh,
        in_specs=(
            P("attn", "expert"),
            P("attn", "expert"),
            P("attn", "expert", None, None),
            P("attn", "expert", None, None),
            P("attn", "expert"),
            P("attn", "expert"),
            P("attn"),
            P("expert"),
            P("expert", None),
            P("attn", None),
            P("expert", None, "attn"),
            P("expert", None, "attn"),
            P("expert", "attn", None),
        ),
        out_specs=P("attn", "expert"),
        check_vma=False,
    )
```

```python
import functools
import math

import jax
import jax.numpy as jnp
from jax import lax
from jax.experimental import pallas as pl
from jax.experimental.pallas import tpu as pltpu
from jax.sharding import PartitionSpec as P

D = 6144
E = 8
CAP = 32
SIDE = 4


EPSILON = 1e-05


def ring_pairs(step, second):
    pairs = []
    for z in range(SIDE):
        for x in range(SIDE):
            for y in range(SIDE):
                for core in range(2):
                    along_z = (core == 0) != second
                    to_z = (z + step) % SIDE if along_z else z
                    to_x = x if along_z else (x + step) % SIDE
                    source = (z * SIDE + x) * E + y * 2 + core
                    target = (to_z * SIDE + to_x) * E + y * 2 + core
                    pairs.append((source, target))
    return pairs


def shift_first(value, step):
    return lax.ppermute(value, ("attn", "expert"), ring_pairs(step, False))


def shift_second(value, step):
    return lax.ppermute(value, ("attn", "expert"), ring_pairs(step, True))


def shift_y(value, step):
    pairs = [
        (y * 2 + core, (y + step) % SIDE * 2 + core) for y in range(SIDE) for core in range(2)
    ]
    return lax.ppermute(value, "expert", pairs)


def swap_cores(value):
    return lax.ppermute(value, "expert", [(index, index ^ 1) for index in range(E)])


def split_three(value):
    high = value.astype(jnp.bfloat16)
    rest = value - high.astype(jnp.float32)
    middle = rest.astype(jnp.bfloat16)
    low = (rest - middle.astype(jnp.float32)).astype(jnp.bfloat16)
    return [high, middle, low]


def add_rounded(one, other):
    return (one.astype(jnp.float32) + other.astype(jnp.float32)).astype(jnp.bfloat16)


CHUNKS = 4
LOAD_VMEM = 24 * 1024 * 1024
FEED_VMEM = 16 * 1024 * 1024


def load_kernel(*refs):
    sources, targets, ready = refs[:3], refs[3:6], refs[6]
    copies = []
    for index, (source, target) in enumerate(zip(sources, targets)):
        part = source.shape[1] // CHUNKS
        for k in range(CHUNKS):
            where = pl.ds(k * part, part)
            copies.append(
                pltpu.make_async_copy(
                    source.at[:, where, :], target.at[:, where, :], ready.at[index, k]
                )
            )
    for copy in copies:
        copy.start()
    for copy in copies:
        copy.wait()


def load(*arrays):
    size = sum(array.size * 2 for array in arrays)
    return pl.pallas_call(
        load_kernel,
        in_specs=[pl.BlockSpec(memory_space=pltpu.HBM)] * 3,
        out_specs=[pl.BlockSpec(memory_space=pltpu.VMEM)] * 3,
        out_shape=[jax.ShapeDtypeStruct(array.shape, array.dtype) for array in arrays],
        scratch_shapes=[pltpu.SemaphoreType.DMA((3, CHUNKS))],
        compiler_params=pltpu.CompilerParams(vmem_limit_bytes=LOAD_VMEM),
        cost_estimate=pl.CostEstimate(flops=0, bytes_accessed=size, transcendentals=0),
    )(*arrays)


def feed_kernel(count, *refs):
    row_refs = refs[:count]
    gate, up, down = refs[count : count + 3]
    out_refs = refs[count + 3 : 2 * count + 3]
    rows = refs[-1]
    width, hidden = gate.shape[1:]
    depth = width // CHUNKS
    at = 0
    for ref in row_refs:
        rows[at : at + ref.shape[0], :] = ref[...]
        at += ref.shape[0]
    gate_sum = jnp.zeros((rows.shape[0], hidden), jnp.float32)
    up_sum = jnp.zeros((rows.shape[0], hidden), jnp.float32)
    for k in range(CHUNKS):
        part = rows[:, k * depth : (k + 1) * depth]
        gate_sum += jnp.dot(
            part, gate[0, k * depth : (k + 1) * depth, :], preferred_element_type=jnp.float32
        )
        up_sum += jnp.dot(
            part, up[0, k * depth : (k + 1) * depth, :], preferred_element_type=jnp.float32
        )
    active = (jax.nn.silu(gate_sum) * up_sum).astype(jnp.bfloat16)
    for k in range(CHUNKS):
        partial = jnp.dot(
            active, down[0, :, k * depth : (k + 1) * depth], preferred_element_type=jnp.float32
        ).astype(jnp.bfloat16)
        at = 0
        for ref in out_refs:
            ref[:, k * depth : (k + 1) * depth] = partial[at : at + ref.shape[0]]
            at += ref.shape[0]


def feed(row_arrays, w_gate, w_up, w_down):
    count = sum(array.shape[0] for array in row_arrays)
    width, hidden = w_gate.shape[1:]
    return pl.pallas_call(
        functools.partial(feed_kernel, len(row_arrays)),
        in_specs=[pl.BlockSpec(memory_space=pltpu.VMEM)] * (len(row_arrays) + 3),
        out_specs=[pl.BlockSpec(memory_space=pltpu.VMEM)] * len(row_arrays),
        out_shape=[jax.ShapeDtypeStruct(array.shape, jnp.bfloat16) for array in row_arrays],
        scratch_shapes=[pltpu.VMEM((count, width), jnp.bfloat16)],
        compiler_params=pltpu.CompilerParams(vmem_limit_bytes=FEED_VMEM),
        cost_estimate=pl.CostEstimate(
            flops=6 * count * width * hidden,
            bytes_accessed=4 * count * width,
            transcendentals=count * hidden,
        ),
    )(*row_arrays, w_gate, w_up, w_down)


def spread_near(block, shift):
    return shift(block, 1), shift(block, -1)


def spread_far(near_up, near_down, shift):
    half = near_up.shape[0] // 2
    return shift(near_up[:half], 1), shift(near_down[half:], -1)


def halves_added(ahead, behind, far_low, far_high, shift):
    half = far_low.shape[0]
    got_low, got_high = shift(far_low, 1), shift(far_high, -1)
    up = ahead.at[:half].set(add_rounded(ahead[:half], got_low))
    down = behind.at[half:].set(add_rounded(behind[half:], got_high))
    return up, down


def add_three(own, one, other):
    total = own.astype(jnp.float32) + one.astype(jnp.float32) + other.astype(jnp.float32)
    return total.astype(jnp.bfloat16)


def on_device(
    resid,
    query,
    key_cache,
    value_cache,
    new_key,
    new_value,
    lengths,
    norm_gain,
    router_weight,
    expert_ids,
    w_gate,
    w_up,
    w_down,
):
    row_count = resid.shape[0]
    width_local = resid.shape[1]
    kv_local = key_cache.shape[1]
    cache_slots = key_cache.shape[2]
    head_size = key_cache.shape[3]
    group_size = query.shape[1] // (kv_local * head_size)
    score_scale = 1.0 / math.sqrt(head_size)
    queries = query.reshape(row_count, kv_local, group_size, head_size)
    scores = (
        jnp.einsum("rkgd,rkld->rkgl", queries, key_cache, preferred_element_type=jnp.float32)
        * score_scale
    )
    fresh_score = (
        jnp.einsum(
            "rkgd,rkd->rkg",
            queries,
            new_key.reshape(row_count, kv_local, head_size),
            preferred_element_type=jnp.float32,
        )
        * score_scale
    )
    usable = lax.broadcasted_iota(jnp.int32, (row_count, cache_slots), 1) < lengths[:, None]
    powers = jnp.where(usable[:, None, None, :], jnp.exp(scores), jnp.float32(0.0))
    fresh_power = jnp.exp(fresh_score)
    denominator = jnp.sum(powers, axis=-1) + fresh_power
    weights_cache = (powers / denominator[..., None]).astype(jnp.bfloat16)
    weight_fresh = (fresh_power / denominator).astype(jnp.bfloat16)
    attended = jnp.einsum(
        "rkgl,rkld->rkgd", weights_cache, value_cache, preferred_element_type=jnp.float32
    )
    attended = attended + weight_fresh.astype(jnp.float32)[..., None] * new_value.astype(
        jnp.float32
    ).reshape(row_count, kv_local, 1, head_size)
    hidden_state = resid.astype(jnp.float32) + attended.reshape(row_count, width_local)

    gained = hidden_state * norm_gain
    sums = jnp.concatenate(
        [
            jnp.sum(hidden_state * hidden_state, axis=1, keepdims=True),
            jnp.dot(gained, router_weight, precision=lax.Precision.HIGHEST),
        ],
        axis=1,
    )
    pieces = split_three(sums)
    columns = sums.shape[1]
    payload = jnp.concatenate(
        [gained.astype(jnp.bfloat16)]
        + pieces
        + [jnp.zeros((row_count, 128 - 3 * columns), jnp.bfloat16)],
        axis=1,
    )
    gathered = lax.all_gather(payload, "expert", axis=0)
    whole_rows = gathered[:, :, :width_local]
    side = gathered[:, :, width_local:].astype(jnp.float32)
    sums = jnp.sum(
        side[:, :, :columns] + side[:, :, columns : 2 * columns] + side[:, :, 2 * columns : 3 * columns],
        axis=0,
    )
    scale = lax.rsqrt(sums[:, :1] / D + EPSILON)
    logits = sums[:, 1:] * scale

    choose = expert_ids[:, :, None] == lax.broadcasted_iota(jnp.int32, (1, 1, E), 2)
    picked = jnp.sum(jnp.where(choose, logits[:, None, :], jnp.float32(0.0)), axis=2)
    first_weight = 1.0 / (1.0 + jnp.exp(picked[:, 1] - picked[:, 0]))
    second_weight = 1.0 / (1.0 + jnp.exp(picked[:, 0] - picked[:, 1]))
    hits = jnp.sum(choose.astype(jnp.int32), axis=1)
    before = jnp.cumsum(hits, axis=0) - hits
    slot_index = jnp.sum(jnp.where(choose, before[:, None, :], 0), axis=2)
    own_expert = lax.axis_index("expert")
    own_slot = jnp.sum(jnp.where(expert_ids == own_expert, slot_index + 1, 0), axis=1) - 1
    own_selector = (
        lax.broadcasted_iota(jnp.int32, (CAP, row_count), 0) == own_slot[None, :]
    )
    outgoing = jnp.einsum(
        "cr,erd->ced",
        own_selector.astype(jnp.bfloat16),
        whole_rows,
        preferred_element_type=jnp.float32,
    ).reshape(CAP, D)
    own_scale = jnp.sum(
        jnp.where(own_selector, scale[:, 0][None, :], jnp.float32(0.0)), axis=1, keepdims=True
    )
    outgoing = (outgoing * own_scale).astype(jnp.bfloat16)

    near = spread_near(outgoing, shift_first)
    line = jnp.concatenate([outgoing, *near, shift_first(outgoing, 2)], axis=0)
    weights = lax.optimization_barrier((w_gate, w_up, w_down, line))[:3]
    weights = load(*weights)
    line_near = spread_near(line, shift_second)
    (own_part,) = feed([line], *weights)
    line_near, own_part = lax.optimization_barrier((line_near, own_part))
    line_far = spread_far(*line_near, shift_second)
    behind_part, ahead_part = feed(line_near, *weights)
    line_far, behind_part, ahead_part = lax.optimization_barrier(
        (line_far, behind_part, ahead_part)
    )
    far_part = feed(line_far, *weights)

    up, down = halves_added(ahead_part, behind_part, *far_part, shift_second)
    line_sum = add_three(own_part, shift_second(up, 1), shift_second(down, -1))
    parts = [line_sum[k * CAP : (k + 1) * CAP] for k in range(SIDE)]
    expert_result = (
        parts[0].astype(jnp.float32)
        + shift_first(parts[1], -1).astype(jnp.float32)
        + shift_first(parts[2], 1).astype(jnp.float32)
        + shift_first(parts[3], 2).astype(jnp.float32)
    ).astype(jnp.bfloat16)

    core = own_expert % 2
    row_y = own_expert // 2
    slices = jnp.swapaxes(expert_result.reshape(CAP, SIDE, 2, width_local), 0, 1)
    even, odd = slices[:, :, 0], slices[:, :, 1]
    kept = jnp.where(core == 0, even, odd)
    swapped = swap_cores(jnp.where(core == 0, odd, even))
    pair = jnp.concatenate([kept, swapped], axis=1)
    blocks = []
    for step in range(SIDE):
        block = lax.dynamic_index_in_dim(pair, (row_y + step) % SIDE, 0, keepdims=False)
        blocks.append(block if step == 0 else shift_y(block, step))
    flat_result = jnp.concatenate(blocks, axis=0)
    away = (row_y - expert_ids // 2 + SIDE) % SIDE
    target_index = (away * 2 + (expert_ids + core) % 2) * CAP + slot_index
    picker = (
        target_index[:, :, None] == lax.broadcasted_iota(jnp.int32, (1, 1, CAP * E), 2)
    ).astype(jnp.bfloat16)
    taken = jnp.einsum("rkm,md->krd", picker, flat_result, preferred_element_type=jnp.float32)
    total = hidden_state + first_weight[:, None] * taken[0] + second_weight[:, None] * taken[1]
    return total.astype(jnp.bfloat16)


def solution(mesh):
    return jax.shard_map(
        on_device,
        mesh=mesh,
        in_specs=(
            P("attn", "expert"),
            P("attn", "expert"),
            P("attn", "expert", None, None),
            P("attn", "expert", None, None),
            P("attn", "expert"),
            P("attn", "expert"),
            P("attn"),
            P("expert"),
            P("expert", None),
            P("attn", None),
            P("expert", None, "attn"),
            P("expert", None, "attn"),
            P("expert", "attn", None),
        ),
        out_specs=P("attn", "expert"),
        check_vma=False,
    )
```

```python
import functools
import math

import jax
import jax.numpy as jnp
from jax import lax
from jax.experimental import pallas as pl
from jax.experimental.pallas import tpu as pltpu
from jax.sharding import PartitionSpec as P

D = 6144
E = 8
CAP = 32
SIDE = 4


EPSILON = 1e-05


def ring_pairs(step, second):
    pairs = []
    for z in range(SIDE):
        for x in range(SIDE):
            for y in range(SIDE):
                for core in range(2):
                    along_z = (core == 1) != second
                    to_z = (z + step) % SIDE if along_z else z
                    to_x = x if along_z else (x + step) % SIDE
                    source = (z * SIDE + x) * E + y * 2 + core
                    target = (to_z * SIDE + to_x) * E + y * 2 + core
                    pairs.append((source, target))
    return pairs


def shift_first(value, step):
    return lax.ppermute(value, ("attn", "expert"), ring_pairs(step, False))


def shift_second(value, step):
    return lax.ppermute(value, ("attn", "expert"), ring_pairs(step, True))


def shift_y(value, step):
    pairs = [
        (y * 2 + core, (y + step) % SIDE * 2 + core) for y in range(SIDE) for core in range(2)
    ]
    return lax.ppermute(value, "expert", pairs)


def swap_cores(value):
    return lax.ppermute(value, "expert", [(index, index ^ 1) for index in range(E)])


def split_three(value):
    high = value.astype(jnp.bfloat16)
    rest = value - high.astype(jnp.float32)
    middle = rest.astype(jnp.bfloat16)
    low = (rest - middle.astype(jnp.float32)).astype(jnp.bfloat16)
    return [high, middle, low]


def add_rounded(one, other):
    return (one.astype(jnp.float32) + other.astype(jnp.float32)).astype(jnp.bfloat16)


CHUNKS = 4
LOAD_VMEM = 24 * 1024 * 1024
FEED_VMEM = 16 * 1024 * 1024


def load_kernel(*refs):
    sources, targets, ready = refs[:3], refs[3:6], refs[6]
    copies = []
    for index, (source, target) in enumerate(zip(sources, targets)):
        part = source.shape[1] // CHUNKS
        for k in range(CHUNKS):
            where = pl.ds(k * part, part)
            copies.append(
                pltpu.make_async_copy(
                    source.at[:, where, :], target.at[:, where, :], ready.at[index, k]
                )
            )
    for copy in copies:
        copy.start()
    for copy in copies:
        copy.wait()


def load(*arrays):
    size = sum(array.size * 2 for array in arrays)
    return pl.pallas_call(
        load_kernel,
        in_specs=[pl.BlockSpec(memory_space=pltpu.HBM)] * 3,
        out_specs=[pl.BlockSpec(memory_space=pltpu.VMEM)] * 3,
        out_shape=[jax.ShapeDtypeStruct(array.shape, array.dtype) for array in arrays],
        scratch_shapes=[pltpu.SemaphoreType.DMA((3, CHUNKS))],
        compiler_params=pltpu.CompilerParams(vmem_limit_bytes=LOAD_VMEM),
        cost_estimate=pl.CostEstimate(flops=0, bytes_accessed=size, transcendentals=0),
    )(*arrays)


def feed_kernel(count, *refs):
    row_refs = refs[:count]
    gate, up, down = refs[count : count + 3]
    out_refs = refs[count + 3 : 2 * count + 3]
    rows = refs[-1]
    width, hidden = gate.shape[1:]
    depth = width // CHUNKS
    at = 0
    for ref in row_refs:
        rows[at : at + ref.shape[0], :] = ref[...]
        at += ref.shape[0]
    gate_sum = jnp.zeros((rows.shape[0], hidden), jnp.float32)
    up_sum = jnp.zeros((rows.shape[0], hidden), jnp.float32)
    for k in range(CHUNKS):
        part = rows[:, k * depth : (k + 1) * depth]
        gate_sum += jnp.dot(
            part, gate[0, k * depth : (k + 1) * depth, :], preferred_element_type=jnp.float32
        )
        up_sum += jnp.dot(
            part, up[0, k * depth : (k + 1) * depth, :], preferred_element_type=jnp.float32
        )
    active = (jax.nn.silu(gate_sum) * up_sum).astype(jnp.bfloat16)
    for k in range(CHUNKS):
        partial = jnp.dot(
            active, down[0, :, k * depth : (k + 1) * depth], preferred_element_type=jnp.float32
        ).astype(jnp.bfloat16)
        at = 0
        for ref in out_refs:
            ref[:, k * depth : (k + 1) * depth] = partial[at : at + ref.shape[0]]
            at += ref.shape[0]


def feed(row_arrays, w_gate, w_up, w_down):
    count = sum(array.shape[0] for array in row_arrays)
    width, hidden = w_gate.shape[1:]
    return pl.pallas_call(
        functools.partial(feed_kernel, len(row_arrays)),
        in_specs=[pl.BlockSpec(memory_space=pltpu.VMEM)] * (len(row_arrays) + 3),
        out_specs=[pl.BlockSpec(memory_space=pltpu.VMEM)] * len(row_arrays),
        out_shape=[jax.ShapeDtypeStruct(array.shape, jnp.bfloat16) for array in row_arrays],
        scratch_shapes=[pltpu.VMEM((count, width), jnp.bfloat16)],
        compiler_params=pltpu.CompilerParams(vmem_limit_bytes=FEED_VMEM),
        cost_estimate=pl.CostEstimate(
            flops=6 * count * width * hidden,
            bytes_accessed=4 * count * width,
            transcendentals=count * hidden,
        ),
    )(*row_arrays, w_gate, w_up, w_down)


def spread_near(block, shift):
    return shift(block, 1), shift(block, -1)


def spread_far(near_up, near_down, shift):
    half = near_up.shape[0] // 2
    return shift(near_up[:half], 1), shift(near_down[half:], -1)


def halves_added(ahead, behind, far_low, far_high, shift):
    half = far_low.shape[0]
    got_low, got_high = shift(far_low, 1), shift(far_high, -1)
    up = ahead.at[:half].set(add_rounded(ahead[:half], got_low))
    down = behind.at[half:].set(add_rounded(behind[half:], got_high))
    return up, down


def add_three(own, one, other):
    total = own.astype(jnp.float32) + one.astype(jnp.float32) + other.astype(jnp.float32)
    return total.astype(jnp.bfloat16)


def on_device(
    resid,
    query,
    key_cache,
    value_cache,
    new_key,
    new_value,
    lengths,
    norm_gain,
    router_weight,
    expert_ids,
    w_gate,
    w_up,
    w_down,
):
    row_count = resid.shape[0]
    width_local = resid.shape[1]
    kv_local = key_cache.shape[1]
    cache_slots = key_cache.shape[2]
    head_size = key_cache.shape[3]
    group_size = query.shape[1] // (kv_local * head_size)
    score_scale = 1.0 / math.sqrt(head_size)
    queries = query.reshape(row_count, kv_local, group_size, head_size)
    scores = (
        jnp.einsum("rkgd,rkld->rkgl", queries, key_cache, preferred_element_type=jnp.float32)
        * score_scale
    )
    fresh_score = (
        jnp.einsum(
            "rkgd,rkd->rkg",
            queries,
            new_key.reshape(row_count, kv_local, head_size),
            preferred_element_type=jnp.float32,
        )
        * score_scale
    )
    usable = lax.broadcasted_iota(jnp.int32, (row_count, cache_slots), 1) < lengths[:, None]
    powers = jnp.where(usable[:, None, None, :], jnp.exp(scores), jnp.float32(0.0))
    fresh_power = jnp.exp(fresh_score)
    denominator = jnp.sum(powers, axis=-1) + fresh_power
    weights_cache = (powers / denominator[..., None]).astype(jnp.bfloat16)
    weight_fresh = (fresh_power / denominator).astype(jnp.bfloat16)
    attended = jnp.einsum(
        "rkgl,rkld->rkgd", weights_cache, value_cache, preferred_element_type=jnp.float32
    )
    attended = attended + weight_fresh.astype(jnp.float32)[..., None] * new_value.astype(
        jnp.float32
    ).reshape(row_count, kv_local, 1, head_size)
    hidden_state = resid.astype(jnp.float32) + attended.reshape(row_count, width_local)

    gained = hidden_state * norm_gain
    sums = jnp.concatenate(
        [
            jnp.sum(hidden_state * hidden_state, axis=1, keepdims=True),
            jnp.dot(gained, router_weight, precision=lax.Precision.HIGHEST),
        ],
        axis=1,
    )
    pieces = split_three(sums)
    columns = sums.shape[1]
    payload = jnp.concatenate(
        [gained.astype(jnp.bfloat16)]
        + pieces
        + [jnp.zeros((row_count, 128 - 3 * columns), jnp.bfloat16)],
        axis=1,
    )
    gathered = lax.all_gather(payload, "expert", axis=0)
    whole_rows = gathered[:, :, :width_local]
    side = gathered[:, :, width_local:].astype(jnp.float32)
    sums = jnp.sum(
        side[:, :, :columns] + side[:, :, columns : 2 * columns] + side[:, :, 2 * columns : 3 * columns],
        axis=0,
    )
    scale = lax.rsqrt(sums[:, :1] / D + EPSILON)
    logits = sums[:, 1:] * scale

    choose = expert_ids[:, :, None] == lax.broadcasted_iota(jnp.int32, (1, 1, E), 2)
    picked = jnp.sum(jnp.where(choose, logits[:, None, :], jnp.float32(0.0)), axis=2)
    first_weight = 1.0 / (1.0 + jnp.exp(picked[:, 1] - picked[:, 0]))
    second_weight = 1.0 / (1.0 + jnp.exp(picked[:, 0] - picked[:, 1]))
    hits = jnp.sum(choose.astype(jnp.int32), axis=1)
    before = jnp.cumsum(hits, axis=0) - hits
    slot_index = jnp.sum(jnp.where(choose, before[:, None, :], 0), axis=2)
    own_expert = lax.axis_index("expert")
    own_slot = jnp.sum(jnp.where(expert_ids == own_expert, slot_index + 1, 0), axis=1) - 1
    own_selector = (
        lax.broadcasted_iota(jnp.int32, (CAP, row_count), 0) == own_slot[None, :]
    )
    outgoing = jnp.einsum(
        "cr,erd->ced",
        own_selector.astype(jnp.bfloat16),
        whole_rows,
        preferred_element_type=jnp.float32,
    ).reshape(CAP, D)
    own_scale = jnp.sum(
        jnp.where(own_selector, scale[:, 0][None, :], jnp.float32(0.0)), axis=1, keepdims=True
    )
    outgoing = (outgoing * own_scale).astype(jnp.bfloat16)

    near = spread_near(outgoing, shift_first)
    line = jnp.concatenate([outgoing, *near, shift_first(outgoing, 2)], axis=0)
    weights = lax.optimization_barrier((w_gate, w_up, w_down, line))[:3]
    weights = load(*weights)
    line_near = spread_near(line, shift_second)
    (own_part,) = feed([line], *weights)
    line_near, own_part = lax.optimization_barrier((line_near, own_part))
    line_far = spread_far(*line_near, shift_second)
    behind_part, ahead_part = feed(line_near, *weights)
    line_far, behind_part, ahead_part = lax.optimization_barrier(
        (line_far, behind_part, ahead_part)
    )
    far_part = feed(line_far, *weights)

    up, down = halves_added(ahead_part, behind_part, *far_part, shift_second)
    line_sum = add_three(own_part, shift_second(up, 1), shift_second(down, -1))
    parts = [line_sum[k * CAP : (k + 1) * CAP] for k in range(SIDE)]
    expert_result = (
        parts[0].astype(jnp.float32)
        + shift_first(parts[1], -1).astype(jnp.float32)
        + shift_first(parts[2], 1).astype(jnp.float32)
        + shift_first(parts[3], 2).astype(jnp.float32)
    ).astype(jnp.bfloat16)

    core = own_expert % 2
    row_y = own_expert // 2
    slices = jnp.swapaxes(expert_result.reshape(CAP, SIDE, 2, width_local), 0, 1)
    even, odd = slices[:, :, 0], slices[:, :, 1]
    kept = jnp.where(core == 0, even, odd)
    swapped = swap_cores(jnp.where(core == 0, odd, even))
    pair = jnp.concatenate([kept, swapped], axis=1)
    blocks = []
    for step in range(SIDE):
        block = lax.dynamic_index_in_dim(pair, (row_y + step) % SIDE, 0, keepdims=False)
        blocks.append(block if step == 0 else shift_y(block, step))
    flat_result = jnp.concatenate(blocks, axis=0)
    away = (row_y - expert_ids // 2 + SIDE) % SIDE
    target_index = (away * 2 + (expert_ids + core) % 2) * CAP + slot_index
    picker = (
        target_index[:, :, None] == lax.broadcasted_iota(jnp.int32, (1, 1, CAP * E), 2)
    ).astype(jnp.bfloat16)
    taken = jnp.einsum("rkm,md->krd", picker, flat_result, preferred_element_type=jnp.float32)
    total = hidden_state + first_weight[:, None] * taken[0] + second_weight[:, None] * taken[1]
    return total.astype(jnp.bfloat16)


def solution(mesh):
    return jax.shard_map(
        on_device,
        mesh=mesh,
        in_specs=(
            P("attn", "expert"),
            P("attn", "expert"),
            P("attn", "expert", None, None),
            P("attn", "expert", None, None),
            P("attn", "expert"),
            P("attn", "expert"),
            P("attn"),
            P("expert"),
            P("expert", None),
            P("attn", None),
            P("expert", None, "attn"),
            P("expert", None, "attn"),
            P("expert", "attn", None),
        ),
        out_specs=P("attn", "expert"),
        check_vma=False,
    )
```

```python
import functools
import math

import jax
import jax.numpy as jnp
from jax import lax
from jax.experimental import pallas as pl
from jax.experimental.pallas import tpu as pltpu
from jax.sharding import PartitionSpec as P

D = 6144
E = 8
CAP = 32
SIDE = 4


EPSILON = 1e-05


def ring_pairs(step, second):
    pairs = []
    for z in range(SIDE):
        for x in range(SIDE):
            for y in range(SIDE):
                for core in range(2):
                    along_z = (core == 1) != second
                    to_z = (z + step) % SIDE if along_z else z
                    to_x = x if along_z else (x + step) % SIDE
                    source = (z * SIDE + x) * E + y * 2 + core
                    target = (to_z * SIDE + to_x) * E + y * 2 + core
                    pairs.append((source, target))
    return pairs


def shift_first(value, step):
    return lax.ppermute(value, ("attn", "expert"), ring_pairs(step, False))


def shift_second(value, step):
    return lax.ppermute(value, ("attn", "expert"), ring_pairs(step, True))


def shift_y(value, step):
    pairs = [
        (y * 2 + core, (y + step) % SIDE * 2 + core) for y in range(SIDE) for core in range(2)
    ]
    return lax.ppermute(value, "expert", pairs)


def swap_cores(value):
    return lax.ppermute(value, "expert", [(index, index ^ 1) for index in range(E)])


def split_three(value):
    high = value.astype(jnp.bfloat16)
    rest = value - high.astype(jnp.float32)
    middle = rest.astype(jnp.bfloat16)
    low = (rest - middle.astype(jnp.float32)).astype(jnp.bfloat16)
    return [high, middle, low]


def add_rounded(one, other):
    return (one.astype(jnp.float32) + other.astype(jnp.float32)).astype(jnp.bfloat16)


CHUNKS = 4
LOAD_VMEM = 24 * 1024 * 1024
FEED_VMEM = 16 * 1024 * 1024


def load_kernel(*refs):
    sources, targets, ready = refs[:3], refs[3:6], refs[6]
    copies = []
    for index, (source, target) in enumerate(zip(sources, targets)):
        part = source.shape[1] // CHUNKS
        for k in range(CHUNKS):
            where = pl.ds(k * part, part)
            copies.append(
                pltpu.make_async_copy(
                    source.at[:, where, :], target.at[:, where, :], ready.at[index, k]
                )
            )
    for copy in copies:
        copy.start()
    for copy in copies:
        copy.wait()


def load(*arrays):
    size = sum(array.size * 2 for array in arrays)
    return pl.pallas_call(
        load_kernel,
        in_specs=[pl.BlockSpec(memory_space=pltpu.HBM)] * 3,
        out_specs=[pl.BlockSpec(memory_space=pltpu.VMEM)] * 3,
        out_shape=[jax.ShapeDtypeStruct(array.shape, array.dtype) for array in arrays],
        scratch_shapes=[pltpu.SemaphoreType.DMA((3, CHUNKS))],
        compiler_params=pltpu.CompilerParams(vmem_limit_bytes=LOAD_VMEM),
        cost_estimate=pl.CostEstimate(flops=0, bytes_accessed=size, transcendentals=0),
    )(*arrays)


def feed_kernel(count, *refs):
    row_refs = refs[:count]
    gate, up, down = refs[count : count + 3]
    out_refs = refs[count + 3 : 2 * count + 3]
    rows = refs[-1]
    width, hidden = gate.shape[1:]
    depth = width // CHUNKS
    at = 0
    for ref in row_refs:
        rows[at : at + ref.shape[0], :] = ref[...]
        at += ref.shape[0]
    gate_sum = jnp.zeros((rows.shape[0], hidden), jnp.float32)
    up_sum = jnp.zeros((rows.shape[0], hidden), jnp.float32)
    for k in range(CHUNKS):
        part = rows[:, k * depth : (k + 1) * depth]
        gate_sum += jnp.dot(
            part, gate[0, k * depth : (k + 1) * depth, :], preferred_element_type=jnp.float32
        )
        up_sum += jnp.dot(
            part, up[0, k * depth : (k + 1) * depth, :], preferred_element_type=jnp.float32
        )
    active = (jax.nn.silu(gate_sum) * up_sum).astype(jnp.bfloat16)
    for k in range(CHUNKS):
        partial = jnp.dot(
            active, down[0, :, k * depth : (k + 1) * depth], preferred_element_type=jnp.float32
        ).astype(jnp.bfloat16)
        at = 0
        for ref in out_refs:
            ref[:, k * depth : (k + 1) * depth] = partial[at : at + ref.shape[0]]
            at += ref.shape[0]


def feed(row_arrays, w_gate, w_up, w_down):
    count = sum(array.shape[0] for array in row_arrays)
    width, hidden = w_gate.shape[1:]
    return pl.pallas_call(
        functools.partial(feed_kernel, len(row_arrays)),
        in_specs=[pl.BlockSpec(memory_space=pltpu.VMEM)] * (len(row_arrays) + 3),
        out_specs=[pl.BlockSpec(memory_space=pltpu.VMEM)] * len(row_arrays),
        out_shape=[jax.ShapeDtypeStruct(array.shape, jnp.bfloat16) for array in row_arrays],
        scratch_shapes=[pltpu.VMEM((count, width), jnp.bfloat16)],
        compiler_params=pltpu.CompilerParams(vmem_limit_bytes=FEED_VMEM),
        cost_estimate=pl.CostEstimate(
            flops=6 * count * width * hidden,
            bytes_accessed=4 * count * width,
            transcendentals=count * hidden,
        ),
    )(*row_arrays, w_gate, w_up, w_down)


def spread_near(block, shift):
    return shift(block, 1), shift(block, -1)


def spread_far(near_up, near_down, shift):
    half = near_up.shape[0] // 2
    return shift(near_up[:half], 1), shift(near_down[half:], -1)


def halves_added(ahead, behind, far_low, far_high, shift):
    half = far_low.shape[0]
    got_low, got_high = shift(far_low, 1), shift(far_high, -1)
    up = ahead.at[:half].set(add_rounded(ahead[:half], got_low))
    down = behind.at[half:].set(add_rounded(behind[half:], got_high))
    return up, down


def add_three(own, one, other):
    total = own.astype(jnp.float32) + one.astype(jnp.float32) + other.astype(jnp.float32)
    return total.astype(jnp.bfloat16)


def on_device(
    resid,
    query,
    key_cache,
    value_cache,
    new_key,
    new_value,
    lengths,
    norm_gain,
    router_weight,
    expert_ids,
    w_gate,
    w_up,
    w_down,
):
    row_count = resid.shape[0]
    width_local = resid.shape[1]
    kv_local = key_cache.shape[1]
    cache_slots = key_cache.shape[2]
    head_size = key_cache.shape[3]
    group_size = query.shape[1] // (kv_local * head_size)
    score_scale = 1.0 / math.sqrt(head_size)
    queries = query.reshape(row_count, kv_local, group_size, head_size)
    scores = (
        jnp.einsum("rkgd,rkld->rkgl", queries, key_cache, preferred_element_type=jnp.float32)
        * score_scale
    )
    fresh_score = (
        jnp.einsum(
            "rkgd,rkd->rkg",
            queries,
            new_key.reshape(row_count, kv_local, head_size),
            preferred_element_type=jnp.float32,
        )
        * score_scale
    )
    usable = lax.broadcasted_iota(jnp.int32, (row_count, cache_slots), 1) < lengths[:, None]
    powers = jnp.where(usable[:, None, None, :], jnp.exp(scores), jnp.float32(0.0))
    fresh_power = jnp.exp(fresh_score)
    denominator = jnp.sum(powers, axis=-1) + fresh_power
    weights_cache = (powers / denominator[..., None]).astype(jnp.bfloat16)
    weight_fresh = (fresh_power / denominator).astype(jnp.bfloat16)
    attended = jnp.einsum(
        "rkgl,rkld->rkgd", weights_cache, value_cache, preferred_element_type=jnp.float32
    )
    attended = attended + weight_fresh.astype(jnp.float32)[..., None] * new_value.astype(
        jnp.float32
    ).reshape(row_count, kv_local, 1, head_size)
    hidden_state = resid.astype(jnp.float32) + attended.reshape(row_count, width_local)

    gained = hidden_state * norm_gain
    sums = jnp.concatenate(
        [
            jnp.sum(hidden_state * hidden_state, axis=1, keepdims=True),
            jnp.dot(gained, router_weight, precision=lax.Precision.HIGHEST),
        ],
        axis=1,
    )
    pieces = split_three(sums)
    columns = sums.shape[1]
    payload = jnp.concatenate(
        [gained.astype(jnp.bfloat16)]
        + pieces
        + [jnp.zeros((row_count, 128 - 3 * columns), jnp.bfloat16)],
        axis=1,
    )
    gathered = lax.all_gather(payload, "expert", axis=0)
    whole_rows = gathered[:, :, :width_local]
    side = gathered[:, :, width_local:].astype(jnp.float32)
    sums = jnp.sum(
        side[:, :, :columns] + side[:, :, columns : 2 * columns] + side[:, :, 2 * columns : 3 * columns],
        axis=0,
    )
    scale = lax.rsqrt(sums[:, :1] / D + EPSILON)
    logits = sums[:, 1:] * scale

    choose = expert_ids[:, :, None] == lax.broadcasted_iota(jnp.int32, (1, 1, E), 2)
    picked = jnp.sum(jnp.where(choose, logits[:, None, :], jnp.float32(0.0)), axis=2)
    first_weight = 1.0 / (1.0 + jnp.exp(picked[:, 1] - picked[:, 0]))
    second_weight = 1.0 / (1.0 + jnp.exp(picked[:, 0] - picked[:, 1]))
    hits = jnp.sum(choose.astype(jnp.int32), axis=1)
    before = jnp.cumsum(hits, axis=0) - hits
    slot_index = jnp.sum(jnp.where(choose, before[:, None, :], 0), axis=2)
    own_expert = lax.axis_index("expert")
    own_slot = jnp.sum(jnp.where(expert_ids == own_expert, slot_index + 1, 0), axis=1) - 1
    own_selector = (
        lax.broadcasted_iota(jnp.int32, (CAP, row_count), 0) == own_slot[None, :]
    )
    outgoing = jnp.einsum(
        "cr,erd->ced",
        own_selector.astype(jnp.bfloat16),
        whole_rows,
        preferred_element_type=jnp.float32,
    ).reshape(CAP, D)
    own_scale = jnp.sum(
        jnp.where(own_selector, scale[:, 0][None, :], jnp.float32(0.0)), axis=1, keepdims=True
    )
    outgoing = (outgoing * own_scale).astype(jnp.bfloat16)

    near = spread_near(outgoing, shift_first)
    line = jnp.concatenate([outgoing, *near, shift_first(outgoing, 2)], axis=0)
    weights = lax.optimization_barrier((w_gate, w_up, w_down, line))[:3]
    weights = load(*weights)
    line_near = spread_near(line, shift_second)
    (own_part,) = feed([line], *weights)
    line_near, own_part = lax.optimization_barrier((line_near, own_part))
    line_far = spread_far(*line_near, shift_second)
    behind_part, ahead_part = feed(line_near, *weights)
    line_far, behind_part, ahead_part = lax.optimization_barrier(
        (line_far, behind_part, ahead_part)
    )
    far_part = feed(line_far, *weights)

    up, down = halves_added(ahead_part, behind_part, *far_part, shift_second)
    line_sum = add_three(own_part, shift_second(up, 1), shift_second(down, -1))
    parts = [line_sum[k * CAP : (k + 1) * CAP] for k in range(SIDE)]
    expert_result = (
        parts[0].astype(jnp.float32)
        + shift_first(parts[1], -1).astype(jnp.float32)
        + shift_first(parts[2], 1).astype(jnp.float32)
        + shift_first(parts[3], 2).astype(jnp.float32)
    ).astype(jnp.bfloat16)

    core = own_expert % 2
    row_y = own_expert // 2
    slices = jnp.swapaxes(expert_result.reshape(CAP, SIDE, 2, width_local), 0, 1)
    even, odd = slices[:, :, 0], slices[:, :, 1]
    kept = jnp.where(core == 0, even, odd)
    swapped = swap_cores(jnp.where(core == 0, odd, even))
    pair = jnp.concatenate([kept, swapped], axis=1)
    blocks = {}
    for step in (0, 1, 3, 2):
        block = lax.dynamic_index_in_dim(pair, (row_y + step) % SIDE, 0, keepdims=False)
        blocks[step] = block if step == 0 else shift_y(block, step)
    flat_result = jnp.concatenate([blocks[step] for step in range(SIDE)], axis=0)
    away = (row_y - expert_ids // 2 + SIDE) % SIDE
    target_index = (away * 2 + (expert_ids + core) % 2) * CAP + slot_index
    picker = (
        target_index[:, :, None] == lax.broadcasted_iota(jnp.int32, (1, 1, CAP * E), 2)
    ).astype(jnp.bfloat16)
    taken = jnp.einsum("rkm,md->krd", picker, flat_result, preferred_element_type=jnp.float32)
    total = hidden_state + first_weight[:, None] * taken[0] + second_weight[:, None] * taken[1]
    return total.astype(jnp.bfloat16)


def solution(mesh):
    return jax.shard_map(
        on_device,
        mesh=mesh,
        in_specs=(
            P("attn", "expert"),
            P("attn", "expert"),
            P("attn", "expert", None, None),
            P("attn", "expert", None, None),
            P("attn", "expert"),
            P("attn", "expert"),
            P("attn"),
            P("expert"),
            P("expert", None),
            P("attn", None),
            P("expert", None, "attn"),
            P("expert", None, "attn"),
            P("expert", "attn", None),
        ),
        out_specs=P("attn", "expert"),
        check_vma=False,
    )
```
